256 devices in a mesh: row: 4 (over y), col: 32 (over x, z), layer: 2 (over core).
Axes of the slice: x: 4, y: 4, z: 8, core: 2. Of those that a mesh axis runs over, the one named last changes fastest.
Arguments:
- xband: bfloat16 [1024, 9, 128, 128], P(('row', 'col')), may hold values from -6 to 6
- xkeep: int32 [1024, 9], P(('row', 'col')), may hold values 0 or 1
- ykeep: int32 [1024, 17], P(('row', 'col')), may hold values 0 or 1
Outputs:
- xnext: bfloat16 [1024, 9, 128, 128], P(('row', 'col'), None, 'layer')
The draws below stay inside these ranges and needn't reach their ends.
All inputs are finite; a program needn't handle non-finite values. No bound on the sum of `xkeep` or of `ykeep` on one device may be relied on, other than what follows from the above.
Results may differ from the reference program's by a relative error of at most 0.0065.
Values may be sent and summed in bfloat16 or wider, within the bound.
A program may use at most 192 MiB of HBM per device.

```python
import jax
import jax.numpy as jnp
from jax import lax

B = 128
W = 4
ROWS_DEV = 8
NB = 1024
N_ROW = 4
N_COL = 32


def place_ends(drawn, key, low, largest):
    extent = drawn.shape
    place = [jax.random.randint(jax.random.fold_in(key, axis), (), 0, extent[axis]) for axis in range(len(extent))]
    drawn = drawn.at[tuple(place)].set(low)
    longest = extent.index(max(extent))
    place[longest] = (place[longest] + 1) % extent[longest]
    return drawn.at[tuple(place)].set(largest)


def block_scale(stream_key, dims, shards, smallest, high):
    loudness = 1.0
    for position, shards_of in shards:
        draws = jax.random.uniform(jax.random.fold_in(jax.random.fold_in(stream_key, 6), position), (shards_of,), jnp.float32, smallest / len(shards), high / len(shards))
        loudness = loudness * jnp.repeat(jnp.exp(draws), dims[position] // shards_of).reshape((-1,) + (1,) * (len(dims) - 1 - position))
    return loudness


def gaussian(own_key, dims, scale, limit, shards=(), kind=jnp.bfloat16):
    gain = block_scale(own_key, dims, shards, -0.22, 0.18) if shards else 1.0
    array = jax.random.normal(own_key, dims, jnp.float32) * scale * gain
    return jnp.minimum(jnp.maximum(array, -limit), limit).astype(kind)


def setup_inputs(seed: int = 0) -> dict:
    key_of = jax.random.split(jax.random.key(seed), 4)
    return {
        "xband": gaussian(key_of[0], (NB, 2 * W + 1, B, B), 1.0, 6.0, ((0, 128),)),
        "xkeep": place_ends((jax.random.randint(key_of[1], (NB, 2 * W + 1), 0, 9) < 8).astype(jnp.int32), jax.random.fold_in(key_of[1], 1), 0, 1),
        "ykeep": place_ends((jax.random.randint(key_of[2], (NB, 4 * W + 1), 0, 4) < 3).astype(jnp.int32), jax.random.fold_in(key_of[2], 1), 0, 1),
    }


def reference(xband, xkeep, ykeep):
    width = 2 * W + 1
    scale = (2.0 * width * B) ** -0.5
    groups = N_ROW * N_COL
    masked = xband * xkeep.astype(jnp.bfloat16)[:, :, None, None]
    xpad = jnp.pad(masked, ((W, W), (0, 0), (0, 0), (0, 0)))

    def square_rows(index):
        start = (index * ROWS_DEV).astype(jnp.int32)
        own = lax.dynamic_slice_in_dim(xpad, start + W, ROWS_DEV, 0).astype(jnp.float32)
        total = jnp.zeros((ROWS_DEV, 2 * width - 1, B, B), jnp.float32)
        for g in range(width):
            near = lax.dynamic_slice_in_dim(xpad, start + g, ROWS_DEV, 0).astype(jnp.float32)
            total = total.at[:, g:g + width].add(jnp.einsum('rab,rkbc->rkac', own[:, g], near))
        keep = lax.dynamic_slice_in_dim(ykeep, start, ROWS_DEV, 0).astype(jnp.float32)
        return (total * scale * keep[:, :, None, None]).astype(jnp.bfloat16)

    square = lax.map(square_rows, jnp.arange(groups, dtype=jnp.int32))
    square = square.reshape((groups * ROWS_DEV, 2 * width - 1, B, B))
    ypad = jnp.pad(square, ((W, W), (0, 0), (0, 0), (0, 0)))

    def cube_rows(index):
        start = (index * ROWS_DEV).astype(jnp.int32)
        own = lax.dynamic_slice_in_dim(xpad, start + W, ROWS_DEV, 0).astype(jnp.float32)
        total = jnp.zeros((ROWS_DEV, width, B, B), jnp.float32)
        for g in range(width):
            near = lax.dynamic_slice_in_dim(ypad, start + g, ROWS_DEV, 0)[:, 2 * W - g:4 * W - g + 1]
            total = total + jnp.einsum('rab,rkbc->rkac', own[:, g], near.astype(jnp.float32))
        keep = lax.dynamic_slice_in_dim(xkeep, start, ROWS_DEV, 0).astype(jnp.float32)
        return ((1.5 * own - 0.5 * scale * total) * keep[:, :, None, None]).astype(jnp.bfloat16)

    result = lax.map(cube_rows, jnp.arange(groups, dtype=jnp.int32))
    return result.reshape((groups * ROWS_DEV, width, B, B))
```

```python
import functools

import jax
import jax.numpy as jnp
from jax import lax
from jax.experimental import pallas as pl
from jax.experimental.pallas import tpu as pltpu
from jax.sharding import PartitionSpec as P

B = 128
W = 4
WIDTH = 2 * W + 1
SUPER = W * B
HALF = B // 2
MESH = pl.DeviceIdType.MESH
BF = jnp.bfloat16
F32 = jnp.float32


def kernel(
    groups, cols, scale,
    x_hbm, xk_hbm, yk_hbm, out_ref,
    dm, do, rnm, rnn, ymo, ymm, ymp, yom, yoo, yon, ynm, yno, ymn,
    acc_mm, acc_mn, acc_ynm, acc_ymn, cs, cm, co, stg, pb, po, xk, yk, ykn, ykv,
    in_sem, k_sem, tri_s, tri_r, mid_s, mid_r, yk_s, yk_r, y_s, y_r, cf_s, cf_r, ca_s, ca_r,
    oa_s, oa_r, om_s, om_r, oa_l, om_l, p_s, p_r,
):
    row, col, l = lax.axis_index("row"), lax.axis_index("col"), lax.axis_index("layer")
    group = row * cols + col
    step = 2 * l - 1

    def device(g, layer):
        g = lax.rem(g + groups, groups)
        return (g // cols, lax.rem(g, cols), layer)

    sib = (row, col, 1 - l)
    facing = device(group + step, 1 - l)
    same = device(group + step, l)
    other = device(group - step, l)
    has_n = jnp.logical_and(group + step >= 0, group + step < groups)
    has_other = jnp.logical_and(group - step >= 0, group - step < groups)

    barrier = pltpu.get_barrier_semaphore()
    pl.semaphore_signal(barrier, inc=1, device_id=sib, device_id_type=MESH)

    @pl.when(has_n)
    def _():
        pl.semaphore_signal(barrier, inc=1, device_id=facing, device_id_type=MESH)

    @pl.when(has_other)
    def _():
        pl.semaphore_signal(barrier, inc=1, device_id=other, device_id_type=MESH)

    b_mo, b_mn, b_om, b_op = 8 * (1 - l), 8 * l, 8 * l, 8 * (1 - l)

    def side(right, q):
        return jnp.where(right, q, 3 - q), jnp.where(right, 8 - q, 0)

    keeps = [pltpu.make_async_copy(xk_hbm, xk, k_sem.at[0]), pltpu.make_async_copy(yk_hbm, yk, k_sem.at[1])]
    for copy in keeps:
        copy.start()
    loads_n, loads_m, loads_o = [], [], []
    for q in range(4):
        i, g = side(l == 1, q)
        rows = pl.ds(pl.multiple_of(i * B, B), B)
        loads_n.append(pltpu.make_async_copy(x_hbm.at[4 * l + i, pl.ds(g, q + 1)], dm.at[pl.ds(g + i, q + 1), rows], in_sem.at[q]))
    for i in range(4):
        rows = pl.ds(i * B, B)
        loads_m.append(pltpu.make_async_copy(x_hbm.at[4 * l + i, pl.ds(4 - i, 4)], dm.at[pl.ds(4, 4), rows], in_sem.at[4 + i]))
    for q in range(4):
        i, g = side(l == 0, q)
        rows = pl.ds(pl.multiple_of(i * B, B), B)
        loads_o.append(pltpu.make_async_copy(x_hbm.at[4 * l + i, pl.ds(g, q + 1)], dm.at[pl.ds(g + i, q + 1), rows], in_sem.at[8 + q]))
    for i in range(4):
        rows = pl.ds(i * B, B)
        loads_o.append(pltpu.make_async_copy(x_hbm.at[4 * (1 - l) + i], do.at[pl.ds(i, WIDTH), rows], in_sem.at[12 + i]))
    for copy in loads_n + loads_m + loads_o:
        copy.start()

    for d in (dm, do):
        for k in range(3):
            d[k, (k + 1) * B:, :] = jnp.zeros((SUPER - (k + 1) * B, B), BF)
            d[9 + k, : (k + 1) * B, :] = jnp.zeros(((k + 1) * B, B), BF)
    for s in range(1, 4):
        k = jnp.where(l == 1, s - 1, 4 - s)
        start = pl.multiple_of(jnp.where(l == 1, s * B, 0), B)
        rnm[k, pl.ds(start, (4 - s) * B), :] = jnp.zeros(((4 - s) * B, B), BF)

    @pl.when(jnp.logical_not(has_n))
    def _():
        rnm[...] = jnp.zeros_like(rnm)
        rnn[...] = jnp.zeros_like(rnn)
        cm[...] = jnp.zeros_like(cm)
        ykv[...] = jnp.zeros_like(ykv)

    @pl.when(jnp.logical_not(has_other))
    def _():
        co[...] = jnp.zeros_like(co)

    for copy in keeps:
        copy.wait()

    def mask(ref, srow, k, i):
        keep = xk[4 * srow + i, k - i].astype(F32)
        rows = pl.ds(pl.multiple_of(i * B, B), B)
        ref[k, rows, :] = ref[k, rows, :] * jnp.full((B, B), keep, F32).astype(BF)

    for copy in loads_n:
        copy.wait()
    for q in range(4):
        i, g = side(l == 1, q)
        for t in range(q + 1):
            mask(dm, l, g + i + t, i)

    tri = []
    for s in (4, 3, 2, 1):
        k = jnp.where(l == 1, 4 - s, s - 1)
        start = pl.multiple_of(jnp.where(l == 1, (4 - s) * B, 0), B)
        rows = pl.ds(start, s * B)
        tri.append(pltpu.make_async_remote_copy(
            dm.at[b_mn + k, rows], rnm.at[k, rows], tri_s.at[s - 1], tri_r.at[s - 1], device_id=facing, device_id_type=MESH))
    mid = [
        pltpu.make_async_remote_copy(
            dm.at[4 + j], rnn.at[j], mid_s.at[j], mid_r.at[j], device_id=facing, device_id_type=MESH)
        for j in range(4)
    ]
    send_yk = pltpu.make_async_remote_copy(yk_hbm, ykv, yk_s, yk_r, device_id=facing, device_id_type=MESH)

    pl.semaphore_wait(barrier, jnp.where(has_n, 3, 1))

    @pl.when(has_n)
    def _():
        for copy in tri:
            copy.start()
        send_yk.start()

    for copy in loads_m:
        copy.wait()
    for i in range(4):
        for j in range(4):
            mask(dm, l, 4 + j, i)
    for copy in loads_o:
        copy.wait()
    for q in range(4):
        i, g = side(l == 0, q)
        for t in range(q + 1):
            mask(dm, l, g + i + t, i)
    for i in range(4):
        for g in range(WIDTH):
            mask(do, 1 - l, g + i, i)

    def cat(ref, base=0):
        return jnp.concatenate([ref[base + j] for j in range(4)], axis=1)

    def dot(a, b):
        return jnp.dot(a, b, preferred_element_type=F32)

    def store_y(dst, value, table, first, h):
        for i in range(4):
            for j in range(4):
                keep = table[first + i, jnp.clip(h + j - i, 0, 4 * W)].astype(F32) * scale
                block = value[i * B:(i + 1) * B, j * B:(j + 1) * B]
                dst[j, i * B:(i + 1) * B, :] = (block * keep).astype(BF)

    def x_mo():
        return cat(dm, b_mo)

    def x_mm():
        return cat(dm, 4)

    def x_mn():
        return cat(dm, b_mn)

    def to_sib(src, dst, index):
        return pltpu.make_async_remote_copy(src, dst, y_s.at[index], y_r.at[index], device_id=sib, device_id_type=MESH)

    send_ymo, send_ymp, send_ymm = to_sib(ymo, yom, 0), to_sib(ymp, yon, 1), to_sib(ymm, yoo, 2)

    store_y(ymo, dot(x_mo(), cat(do, 4)) + dot(x_mm(), x_mo()), yk, 4 * l, 12 - 8 * l)
    send_ymo.start()
    store_y(ymp, dot(x_mo(), cat(do, b_op)), yk, 4 * l, 16 - 16 * l)
    send_ymp.start()
    acc_ymn[...] = dot(x_mm(), x_mn())
    acc_mm[...] = dot(x_mo(), cat(do, b_om)) + dot(x_mm(), x_mm())

    @pl.when(has_n)
    def _():
        for copy in tri:
            copy.wait_send()
        for copy in mid:
            copy.start()
        send_yk.wait()
        for copy in tri:
            copy.wait_recv()

    to_smem = pltpu.make_async_copy(ykv, ykn, k_sem.at[0])
    to_smem.start()
    store_y(ymm, acc_mm[...] + dot(x_mn(), cat(rnm)), yk, 4 * l, 8)
    send_ymm.start()
    c = dot(cat(rnm), cat(ymm))
    for j in range(4):
        for i in range(4):
            block = c[i * B:(i + 1) * B, j * B:(j + 1) * B].astype(BF)
            for h in range(2):
                cs[h, j, i * HALF:(i + 1) * HALF, :] = block[h * HALF:(h + 1) * HALF]
    to_smem.wait()
    store_y(yno, dot(cat(rnm), x_mo()), ykn, 4 * (1 - l), 16 - 16 * l)
    acc_ynm[...] = dot(cat(rnm), x_mm())

    c_facing, c_same = [], []
    for s in (4, 3, 2, 1):
        j = jnp.where(l == 1, s - 1, 4 - s)
        rows = pl.ds(pl.multiple_of(jnp.where(l == 1, 0, (4 - s) * HALF), HALF), s * HALF)
        c_facing.append(pltpu.make_async_remote_copy(
            cs.at[1 - l, j, rows], cm.at[j, rows], cf_s.at[s - 1], cf_r.at[s - 1], device_id=facing, device_id_type=MESH))
        c_same.append(pltpu.make_async_remote_copy(
            cs.at[l, j, rows], co.at[j, rows], ca_s.at[s - 1], ca_r.at[s - 1], device_id=same, device_id_type=MESH))

    def finish(value, base, i, j):
        keep = xk[4 * l + i, jnp.clip(base + j - i, 0, 2 * W)].astype(F32)
        own = dm[base + j, i * B:(i + 1) * B, :].astype(F32)
        cube = value[i * B:(i + 1) * B, j * B:(j + 1) * B]
        return ((1.5 * own - (0.5 * scale) * cube) * keep).astype(BF)

    def stage(value, base):
        for i in range(4):
            for j in range(4):
                block = finish(value, base, i, j)
                for h in range(2):
                    stg[h, i, 3 + base + j - i] = block[h * HALF:(h + 1) * HALF]

    def outs(i, e, count, send, recv, local):
        there = out_ref.at[4 * l + i, pl.ds(e, count)]
        return (
            pltpu.make_async_remote_copy(stg.at[1 - l, i, pl.ds(3 + e, count)], there, send, recv, device_id=sib, device_id_type=MESH),
            pltpu.make_async_copy(stg.at[l, i, pl.ds(3 + e, count)], there, local),
        )

    send_ymm.wait_recv()
    send_ymo.wait_recv()
    send_ymp.wait_recv()
    stage(dot(x_mo(), cat(yoo)) + dot(x_mm(), cat(ymo)) + dot(x_mn(), cat(yno)), b_mo)
    out_a = []
    for q in range(4):
        i, e = side(l == 0, q)
        out_a.append(outs(i, e, q + 1, oa_s.at[q], oa_r.at[q], oa_l.at[q]))
    for pair in out_a:
        for copy in pair:
            copy.start()
    acc_mm[...] = dot(x_mo(), cat(yom)) + dot(x_mm(), cat(ymm))
    acc_mn[...] = dot(x_mo(), cat(yon))

    @pl.when(has_n)
    def _():
        for copy in mid:
            copy.wait_send()
        for a, b in zip(c_facing, c_same):
            a.start()
            b.start()
        for copy in mid:
            copy.wait_recv()

    store_y(ymn, acc_ymn[...] + dot(x_mn(), cat(rnn)), yk, 4 * l, 4 + 8 * l)
    value = acc_mn[...] + dot(x_mm(), cat(ymn))
    for j in range(4):
        for i in range(4):
            block = finish(value, b_mn, i, j)
            for h in range(2):
                pb[h, j, i * HALF:(i + 1) * HALF, :] = block[h * HALF:(h + 1) * HALF]
    send_p = pltpu.make_async_remote_copy(pb.at[1 - l], po, p_s, p_r, device_id=sib, device_id_type=MESH)
    send_p.start()
    store_y(ynm, acc_ynm[...] + dot(cat(rnn), cat(rnm)), ykn, 4 * (1 - l), 12 - 8 * l)
    stage(acc_mm[...] + dot(x_mn(), cat(ynm)), 4)
    out_m = [outs(i, 4 - i, 4, om_s.at[i], om_r.at[i], om_l.at[i]) for i in range(4)]
    for pair in out_m:
        for copy in pair:
            copy.start()

    send_p.wait_recv()

    def add(srow, part, term, s):
        for t in range(s):
            j = jnp.where(srow == 1, 4 - s, s - 1)
            i = jnp.where(srow == 1, 4 - s + t, t)
            e = jnp.where(srow == 1, 8 + j - i, j - i)
            rows = pl.ds(pl.multiple_of(i * HALF, HALF), HALF)
            keep = xk[4 * srow + i, e].astype(F32) * (0.5 * scale)
            out_ref[4 * srow + i, e] = (part[j, rows, :].astype(F32) - keep * term[j, rows, :].astype(F32)).astype(BF)

    mine = pb.at[l]
    for a, b, s in zip(c_facing, c_same, (4, 3, 2, 1)):

        @pl.when(has_n)
        def _(a=a):
            a.wait_recv()

        add(l, mine, cm, s)

        @pl.when(has_other)
        def _(b=b):
            b.wait_recv()

        add(1 - l, po, co, s)

    for remote, local in out_a + out_m:
        local.wait()
        remote.wait()
    for copy in (send_ymo, send_ymp, send_ymm, send_p):
        copy.wait_send()

    @pl.when(has_n)
    def _():
        for copy in c_facing + c_same:
            copy.wait_send()


def solution(mesh):
    cols = mesh.shape["col"]
    groups = mesh.shape["row"] * cols

    def step(xband, xkeep, ykeep):
        scale = (2.0 * WIDTH * B) ** -0.5
        rows = xband.shape[0]
        dense = lambda n, dtype=BF: pltpu.VMEM((n, SUPER, B), dtype)
        total = pltpu.VMEM((SUPER, SUPER), F32)
        sems = lambda n: pltpu.SemaphoreType.DMA((n,))
        one = pltpu.SemaphoreType.DMA(())
        scratch = (
            [dense(12), dense(12)] + [dense(4)] * 11 + [total] * 4
            + [pltpu.VMEM((2, 4, 4 * HALF, B), BF), pltpu.VMEM((4, 4 * HALF, B), BF), pltpu.VMEM((4, 4 * HALF, B), BF)]
            + [pltpu.VMEM((2, 4, 15, HALF, B), BF), pltpu.VMEM((2, 4, 4 * HALF, B), BF), pltpu.VMEM((4, 4 * HALF, B), BF)]
            + [pltpu.SMEM(xkeep.shape, jnp.int32), pltpu.SMEM(ykeep.shape, jnp.int32), pltpu.SMEM(ykeep.shape, jnp.int32)]
            + [pltpu.VMEM(ykeep.shape, jnp.int32)]
            + [sems(16), sems(2), sems(4), sems(4), sems(4), sems(4), one, one, sems(3), sems(3)]
            + [sems(4)] * 4 + [sems(4)] * 6 + [one, one]
        )
        return pl.pallas_call(
            functools.partial(kernel, groups, cols, scale),
            out_shape=jax.ShapeDtypeStruct((rows, WIDTH, HALF, B), BF),
            in_specs=[pl.BlockSpec(memory_space=pl.ANY)] * 3,
            out_specs=pl.BlockSpec(memory_space=pltpu.VMEM),
            scratch_shapes=scratch,
            compiler_params=pltpu.CompilerParams(
                collective_id=0, has_side_effects=True, vmem_limit_bytes=40 * 2**20),
        )(xband, xkeep, ykeep)

    in_specs = (P(("row", "col"), None, None, None), P(("row", "col"), None), P(("row", "col"), None))
    return jax.shard_map(step, mesh=mesh, in_specs=in_specs, out_specs=P(("row", "col"), None, "layer", None), check_vma=False)
```

```python
import functools

import jax
import jax.numpy as jnp
from jax import lax
from jax.experimental import pallas as pl
from jax.experimental.pallas import tpu as pltpu
from jax.sharding import PartitionSpec as P

B = 128
W = 4
WIDTH = 2 * W + 1
SUPER = W * B
HALF = B // 2
MESH = pl.DeviceIdType.MESH
BF = jnp.bfloat16
F32 = jnp.float32


def kernel(
    groups, cols, scale,
    x_hbm, xk_hbm, yk_hbm, out_ref,
    dm, do, rnm, rnn, ymo, ymm, ymp, yom, yoo, yon, ynm, yno, ymn,
    acc_mm, acc_mn, acc_ynm, acc_ymn, acc_z, zs, zr, yz, cs, cm, co, stg, pb, po, xk, yk, xkn, ykn, xkv, ykv,
    in_sem, k_sem, tri_s, tri_r, mid_s, mid_r, key_s, key_r, y_s, y_r, z_s, z_r, c_s, c_r,
    o_s, o_r, o_l, p_s, p_r,
):
    row, col, l = lax.axis_index("row"), lax.axis_index("col"), lax.axis_index("layer")
    group = row * cols + col
    step = 2 * l - 1

    def device(g, layer):
        g = lax.rem(g + groups, groups)
        return (g // cols, lax.rem(g, cols), layer)

    sib = (row, col, 1 - l)
    facing = device(group + step, 1 - l)
    same = device(group + step, l)
    other = device(group - step, l)
    has_n = jnp.logical_and(group + step >= 0, group + step < groups)
    has_other = jnp.logical_and(group - step >= 0, group - step < groups)

    barrier = pltpu.get_barrier_semaphore()
    pl.semaphore_signal(barrier, inc=1, device_id=sib, device_id_type=MESH)

    @pl.when(has_n)
    def _():
        pl.semaphore_signal(barrier, inc=1, device_id=facing, device_id_type=MESH)

    @pl.when(has_other)
    def _():
        pl.semaphore_signal(barrier, inc=1, device_id=other, device_id_type=MESH)

    b_mo, b_mn, b_om, b_op = 8 * (1 - l), 8 * l, 8 * l, 8 * (1 - l)

    def side(right, q):
        return jnp.where(right, q, 3 - q), jnp.where(right, 8 - q, 0)

    keeps = [pltpu.make_async_copy(xk_hbm, xk, k_sem.at[0]), pltpu.make_async_copy(yk_hbm, yk, k_sem.at[1])]
    loads = [
        pltpu.make_async_copy(x_hbm.at[4 * s + i], d.at[pl.ds(i, WIDTH), pl.ds(i * B, B)], in_sem.at[n, i])
        for n, (s, d) in enumerate(((l, dm), (1 - l, do)))
        for i in range(4)
    ]
    for copy in keeps + loads:
        copy.start()

    keys = [
        pltpu.make_async_remote_copy(src, dst, key_s.at[n], key_r.at[n], device_id=facing, device_id_type=MESH)
        for n, (src, dst) in enumerate(((xk_hbm, xkv), (yk_hbm, ykv)))
    ]
    tri, mid = [], []
    for q in range(4):
        i, e = side(l == 1, q)
        rows = pl.ds(pl.multiple_of(i * B, B), B)
        tri.append(pltpu.make_async_remote_copy(
            x_hbm.at[4 * l + i, pl.ds(e, q + 1)], rnm.at[pl.ds(jnp.where(l == 1, 0, i), q + 1), rows],
            tri_s.at[q], tri_r.at[q], device_id=facing, device_id_type=MESH))
    for i in range(4):
        mid.append(pltpu.make_async_remote_copy(
            x_hbm.at[4 * l + i, pl.ds(4 - i, 4)], rnn.at[:, pl.ds(i * B, B)],
            mid_s.at[i], mid_r.at[i], device_id=facing, device_id_type=MESH))

    @pl.when(jnp.logical_not(has_n))
    def _():
        rnm[...] = jnp.zeros_like(rnm)
        rnn[...] = jnp.zeros_like(rnn)
        zr[...] = jnp.zeros_like(zr)
        cm[...] = jnp.zeros_like(cm)
        xkv[...] = jnp.zeros_like(xkv)
        ykv[...] = jnp.zeros_like(ykv)

    @pl.when(jnp.logical_not(has_other))
    def _():
        co[...] = jnp.zeros_like(co)

    pl.semaphore_wait(barrier, jnp.where(has_n, 3, 1))

    @pl.when(has_n)
    def _():
        for copy in keys + tri[3:] + tri[2:3]:
            copy.start()

    for d in (dm, do):
        for k in range(3):
            d[k, (k + 1) * B:, :] = jnp.zeros((SUPER - (k + 1) * B, B), BF)
            d[9 + k, : (k + 1) * B, :] = jnp.zeros(((k + 1) * B, B), BF)
    for s in range(1, 4):
        k = jnp.where(l == 1, s - 1, 4 - s)
        start = pl.multiple_of(jnp.where(l == 1, s * B, 0), B)
        rnm[k, pl.ds(start, (4 - s) * B), :] = jnp.zeros(((4 - s) * B, B), BF)

    def mask(ref, k, i, keep):
        rows = pl.ds(i * B if isinstance(i, int) else pl.multiple_of(i * B, B), B)
        ref[k, rows, :] = ref[k, rows, :] * jnp.full((B, B), keep.astype(F32), F32).astype(BF)

    for copy in keeps + loads:
        copy.wait()
    for s, d in ((l, dm), (1 - l, do)):
        for i in range(4):
            for g in range(WIDTH):
                mask(d, g + i, i, xk[4 * s + i, g])

    @pl.when(has_n)
    def _():
        tri[2].wait_send()
        for copy in tri[1::-1] + mid[:1]:
            copy.start()

    def cat(ref, base=0, count=4, rows=slice(None)):
        return jnp.concatenate([ref[base + j, rows, :] for j in range(count)], axis=1)

    def lhs(*pieces):
        return jnp.concatenate([cat(*p) for p in pieces], axis=1)

    def rhs(*pieces):
        return jnp.concatenate([cat(*p) for p in pieces], axis=0)

    def dot(a, b):
        return jnp.dot(a, b, preferred_element_type=F32)

    def put(ref, value):
        for j in range(value.shape[1] // B):
            ref[j] = value[:, j * B:(j + 1) * B]

    def store_y(dst, value, table, first, h, base=0, col=0):
        for i in range(4):
            for j in range(value.shape[1] // B):
                keep = table[first + i, jnp.clip(h + col + j - i, 0, 4 * W)].astype(F32) * scale
                block = value[i * B:(i + 1) * B, j * B:(j + 1) * B]
                dst[base + j, i * B:(i + 1) * B, :] = (block * keep).astype(BF)

    def to_sib(src, dst, index):
        return pltpu.make_async_remote_copy(src, dst, y_s.at[index], y_r.at[index], device_id=sib, device_id_type=MESH)

    send_ymo, send_ymp, send_ymm = to_sib(ymo, yom, 0), to_sib(ymp, yon, 1), to_sib(ymm, yoo, 2)
    mo, mm, mn = (dm, b_mo), (dm, 4), (dm, b_mn)
    theirs = 4 * (1 - l)
    z_out, c_out = 2 * l, 2 * (1 - l)
    z_in, c_in = 2 * (1 - l), 2 * l
    send_z = pltpu.make_async_remote_copy(zs, zr, z_s, z_r, device_id=facing, device_id_type=MESH)

    put(acc_mm, dot(lhs(mo, mm), rhs((do, b_om), mm)))
    for j in range(2):
        zs[j] = acc_mm[z_out + j].astype(BF)
    store_y(ymo, dot(lhs(mo, mm), rhs((do, 4), mo)), yk, 4 * l, 12 - 8 * l)
    send_ymo.start()
    store_y(ymp, dot(cat(*mo), cat(do, b_op)), yk, 4 * l, 16 - 16 * l)
    send_ymp.start()

    @pl.when(has_n)
    def _():
        for copy in mid[1:]:
            copy.start()
        for copy in keys:
            copy.wait()

    to_smem = [pltpu.make_async_copy(xkv, xkn, k_sem.at[0]), pltpu.make_async_copy(ykv, ykn, k_sem.at[1])]
    for copy in to_smem:
        copy.start()
    put(acc_ymn, dot(cat(*mm), cat(*mn)))
    for copy in to_smem:
        copy.wait()

    @pl.when(has_n)
    def _():
        mid[0].wait_send()
        send_z.start()

    def mask_tri(q):
        i, e = side(l == 0, q)
        for t in range(q + 1):
            mask(rnm, jnp.where(l == 0, 0, i) + t, i, xkn[theirs + i, e + t])

    @pl.when(has_n)
    def _():
        for copy in tri[2:]:
            copy.wait_recv()

    mask_tri(3)
    mask_tri(2)
    pair = pl.ds(pl.multiple_of(c_out * B, B), 2 * B)
    value = cat(acc_mm, c_out, 2) + dot(cat(dm, b_mn + c_out, 2), cat(rnm, c_out, 2, pair))
    store_y(ymm, value, yk, 4 * l, 8, c_out, c_out)
    c = dot(cat(rnm, 0, 4, pair), cat(ymm, c_out, 2))
    for j in range(2):
        for i in range(2):
            block = c[i * B:(i + 1) * B, j * B:(j + 1) * B].astype(BF)
            slot = jnp.where(l == 1, (2, 0, 3, 1)[2 * i + j], (0, 3, 1, 2)[2 * i + j])
            for h in range(2):
                cs[h, slot] = block[h * HALF:(h + 1) * HALF]
    c_facing, c_same = [
        pltpu.make_async_remote_copy(
            cs.at[h, pl.ds(0, 3)], dst, c_s.at[n], c_r.at[n], device_id=there, device_id_type=MESH)
        for n, (h, dst, there) in enumerate(((1 - l, cm, facing), (l, co, same)))
    ]

    @pl.when(has_n)
    def _():
        c_facing.start()
        c_same.start()
        for copy in tri[:2]:
            copy.wait_recv()

    mask_tri(1)
    mask_tri(0)
    store_y(ymm, cat(acc_mm, z_out, 2) + dot(cat(*mn), cat(rnm, z_out, 2)), yk, 4 * l, 8, z_out, z_out)
    send_ymm.start()
    store_y(yno, dot(cat(rnm), cat(*mo)), ykn, theirs, 16 - 16 * l)
    put(acc_ynm, dot(cat(rnm), cat(*mm)))
    put(acc_z, dot(cat(rnm), cat(dm, b_mn + z_in, 2)))

    def finish(cube, base, i, j):
        keep = xk[4 * l + i, jnp.clip(base + j - i, 0, 2 * W)].astype(F32)
        rows = pl.ds(i * B if isinstance(i, int) else pl.multiple_of(i * B, B), B)
        own = dm[base + j, rows, :].astype(F32)
        return ((1.5 * own - (0.5 * scale) * cube) * keep).astype(BF)

    def stage(value, base):
        for i in range(4):
            for j in range(value.shape[1] // B):
                block = finish(value[i * B:(i + 1) * B, j * B:(j + 1) * B], base, i, j)
                for h in range(2):
                    stg[h, i, 3 + base + j - i] = block[h * HALF:(h + 1) * HALF]

    def outs(n, i, e, count):
        there = out_ref.at[4 * l + i, pl.ds(e, count)]
        return [
            pltpu.make_async_remote_copy(
                stg.at[1 - l, i, pl.ds(3 + e, count)], there, o_s.at[n], o_r.at[n], device_id=sib, device_id_type=MESH),
            pltpu.make_async_copy(stg.at[l, i, pl.ds(3 + e, count)], there, o_l.at[n]),
        ]

    send_ymo.wait_recv()
    send_ymp.wait_recv()
    put(acc_mn, dot(cat(*mo), cat(yon)))
    send_ymm.wait_recv()
    stage(dot(lhs(mo, mm, mn), rhs((yoo,), (ymo,), (yno,))), b_mo)
    out_a = []
    for q in range(4):
        i, e = side(l == 0, q)
        out_a += outs(q, i, e, q + 1)
    for copy in out_a:
        copy.start()
    put(acc_mm, dot(lhs(mo, mm), rhs((yom,), (ymm,))))

    @pl.when(has_n)
    def _():
        for copy in mid:
            copy.wait_recv()

    for i in range(4):
        for j in range(4):
            mask(rnn, j, i, xkn[theirs + i, 4 + j - i])
    store_y(ymn, cat(acc_ymn) + dot(cat(*mn), cat(rnn)), yk, 4 * l, 4 + 8 * l)
    pair = pl.ds(pl.multiple_of(c_in * B, B), 2 * B)
    value = cat(acc_mn, c_in, 2, pair) + dot(cat(dm, 4, 4, pair), cat(ymn, c_in, 2))
    for j in range(2):
        for i in range(2):
            block = finish(value[i * B:(i + 1) * B, j * B:(j + 1) * B], b_mn, c_in + i, c_in + j)
            slot = jnp.where(l == 0, (2, 0, 3, 1)[2 * i + j], (0, 3, 1, 2)[2 * i + j])
            for h in range(2):
                pb[h, slot] = block[h * HALF:(h + 1) * HALF]
    send_p = pltpu.make_async_remote_copy(pb.at[1 - l, pl.ds(0, 3)], po, p_s, p_r, device_id=sib, device_id_type=MESH)
    send_p.start()
    store_y(ynm, cat(acc_ynm) + dot(cat(rnn), cat(rnm)), ykn, theirs, 12 - 8 * l)
    stage(cat(acc_mm) + dot(cat(*mn), cat(ynm)), 4)
    out_m = []
    for i in range(4):
        out_m += outs(4 + i, i, 4 - i, 4)
    for copy in out_m:
        copy.start()
    value = cat(acc_mn, z_in, 2) + dot(cat(*mm), cat(ymn, z_in, 2))

    @pl.when(has_n)
    def _():
        send_z.wait_recv()

    store_y(yz, cat(zr, 0, 2).astype(F32) + cat(acc_z, 0, 2), ykn, theirs, 8, 0, z_in)
    stage(value + dot(cat(*mn), cat(yz, 0, 2)), b_mn + z_in)
    out_z = outs(8, jnp.where(l == 1, 0, 3), jnp.where(l == 1, 8, 0), 1)
    for q in range(1, 4):
        out_z += outs(8 + q, jnp.where(l == 1, q, 3 - q), jnp.where(l == 1, 8 - q, q - 1), 2)
    for copy in out_z:
        copy.start()

    send_p.wait_recv()

    def add(srow, part, term):
        for slot in range(3):
            i = jnp.where(srow == 1, (2, 3, 3)[slot], (0, 1, 0)[slot])
            e = jnp.where(srow == 1, (8, 7, 8)[slot], (1, 0, 0)[slot])
            keep = xk[4 * srow + i, e].astype(F32) * (0.5 * scale)
            out_ref[4 * srow + i, e] = (part[slot].astype(F32) - keep * term[slot].astype(F32)).astype(BF)

    @pl.when(has_n)
    def _():
        c_facing.wait_recv()

    add(l, pb.at[l], cm)

    @pl.when(has_other)
    def _():
        c_same.wait_recv()

    add(1 - l, po, co)

    for copy in out_a + out_m + out_z:
        copy.wait()
    for copy in (send_ymo, send_ymp, send_ymm, send_p):
        copy.wait_send()

    @pl.when(has_n)
    def _():
        for copy in tri[:2] + tri[3:] + mid[1:] + [send_z, c_facing, c_same]:
            copy.wait_send()


def solution(mesh):
    cols = mesh.shape["col"]
    groups = mesh.shape["row"] * cols

    def step(xband, xkeep, ykeep):
        scale = (2.0 * WIDTH * B) ** -0.5
        rows = xband.shape[0]
        dense = lambda n, dtype=BF: pltpu.VMEM((n, SUPER, B), dtype)
        sems = lambda *n: pltpu.SemaphoreType.DMA(n)
        halves = lambda *n: pltpu.VMEM((*n, HALF, B), BF)
        scratch = (
            [dense(12), dense(12)] + [dense(4)] * 11 + [dense(4, F32)] * 4 + [dense(2, F32)] + [dense(2)] * 3
            + [halves(2, 4), halves(3), halves(3), halves(2, 4, 15), halves(2, 4), halves(3)]
            + [pltpu.SMEM(a.shape, jnp.int32) for a in (xkeep, ykeep, xkeep, ykeep)]
            + [pltpu.VMEM(a.shape, jnp.int32) for a in (xkeep, ykeep)]
            + [sems(2, 4), sems(2), sems(4), sems(4), sems(4), sems(4), sems(2), sems(2), sems(3), sems(3)]
            + [sems(), sems(), sems(2), sems(2), sems(12), sems(12), sems(12), sems(), sems()]
        )
        args = [pltpu.with_memory_space_constraint(a, pltpu.HBM) for a in (xband, xkeep, ykeep)]
        return pl.pallas_call(
            functools.partial(kernel, groups, cols, scale),
            out_shape=jax.ShapeDtypeStruct((rows, WIDTH, HALF, B), BF),
            in_specs=[pl.BlockSpec(memory_space=pl.ANY)] * 3,
            out_specs=pl.BlockSpec(memory_space=pltpu.VMEM),
            scratch_shapes=scratch,
            compiler_params=pltpu.CompilerParams(
                collective_id=0, has_side_effects=True, vmem_limit_bytes=40 * 2**20),
        )(*args)

    in_specs = (P(("row", "col"), None, None, None), P(("row", "col"), None), P(("row", "col"), None))
    return jax.shard_map(step, mesh=mesh, in_specs=in_specs, out_specs=P(("row", "col"), None, "layer", None), check_vma=False)
```

```python
import functools

import jax
import jax.numpy as jnp
from jax import lax
from jax.experimental import pallas as pl
from jax.experimental.pallas import tpu as pltpu
from jax.sharding import PartitionSpec as P

B = 128
W = 4
LAST = 7
NC = 3
NZ = W - NC
PAIRS = [(a, b) for a in range(W) for b in range(a + 1)]
NP = NC * (NC + 1) // 2
WIDTH = 2 * W + 1
SUPER = W * B
HALF = B // 2
MESH = pl.DeviceIdType.MESH
BF = jnp.bfloat16
F32 = jnp.float32


def kernel(
    groups, cols, scale,
    x_hbm, xk_hbm, yk_hbm, out_ref,
    dm, do, rnm, rnn, ymo, ymm, ymp, yom, yoo, yon, ynm, yno, ymn,
    acc_mm, acc_mn, acc_o, acc_mo, acc_ynm, acc_ymn, acc_z, zs, zr, yz, cs, cm, co, stg, pb, po, xk, yk, xkn, ykn, xkv, ykv,
    in_sem, k_sem, tri_s, tri_r, mid_s, mid_r, key_s, key_r, y_s, y_r, z_s, z_r, c_s, c_r,
    o_s, o_r, p_s, p_r,
):
    row, col, l = lax.axis_index("row"), lax.axis_index("col"), lax.axis_index("layer")
    group = row * cols + col
    step = 2 * l - 1

    def device(g, layer):
        g = lax.rem(g + groups, groups)
        return (g // cols, lax.rem(g, cols), layer)

    sib = (row, col, 1 - l)
    facing = device(group + step, 1 - l)
    same = device(group + step, l)
    other = device(group - step, l)
    has_n = jnp.logical_and(group + step >= 0, group + step < groups)
    has_other = jnp.logical_and(group - step >= 0, group - step < groups)

    early = jnp.logical_and(has_n, jnp.logical_and(l == 0, lax.rem(col, LAST + 1) == 0))
    late = jnp.logical_and(has_n, jnp.logical_and(l == 1, lax.rem(col, LAST + 1) == LAST))

    barrier = pltpu.get_barrier_semaphore()
    pl.semaphore_signal(barrier, inc=1, device_id=sib, device_id_type=MESH)

    @pl.when(has_n)
    def _():
        pl.semaphore_signal(barrier, inc=1, device_id=facing, device_id_type=MESH)

    @pl.when(has_other)
    def _():
        pl.semaphore_signal(barrier, inc=1, device_id=other, device_id_type=MESH)

    b_mo, b_mn, b_om, b_op = 8 * (1 - l), 8 * l, 8 * l, 8 * (1 - l)

    def side(right, q):
        return jnp.where(right, q, 3 - q), jnp.where(right, 8 - q, 0)

    keeps = [pltpu.make_async_copy(xk_hbm, xk, k_sem.at[0]), pltpu.make_async_copy(yk_hbm, yk, k_sem.at[1])]
    loads = [
        pltpu.make_async_copy(x_hbm.at[4 * s + i], d.at[pl.ds(i, WIDTH), pl.ds(i * B, B)], in_sem.at[n, i])
        for n, (s, d) in enumerate(((l, dm), (1 - l, do)))
        for i in range(4)
    ]
    for copy in keeps + loads:
        copy.start()

    keys = [
        pltpu.make_async_remote_copy(src, dst, key_s.at[n], key_r.at[n], device_id=facing, device_id_type=MESH)
        for n, (src, dst) in enumerate(((xk_hbm, xkv), (yk_hbm, ykv)))
    ]
    tri, mid = [], []
    for q in range(4):
        i, e = side(l == 1, q)
        rows = pl.ds(pl.multiple_of(i * B, B), B)
        tri.append(pltpu.make_async_remote_copy(
            x_hbm.at[4 * l + i, pl.ds(e, q + 1)], rnm.at[pl.ds(jnp.where(l == 1, 0, i), q + 1), rows],
            tri_s.at[q], tri_r.at[q], device_id=facing, device_id_type=MESH))
    for i in range(4):
        mid.append(pltpu.make_async_remote_copy(
            x_hbm.at[4 * l + i, pl.ds(4 - i, 4)], rnn.at[:, pl.ds(i * B, B)],
            mid_s.at[i], mid_r.at[i], device_id=facing, device_id_type=MESH))

    @pl.when(jnp.logical_not(has_n))
    def _():
        rnm[...] = jnp.zeros_like(rnm)
        rnn[...] = jnp.zeros_like(rnn)
        zr[...] = jnp.zeros_like(zr)
        cm[...] = jnp.zeros_like(cm)
        xkv[...] = jnp.zeros_like(xkv)
        ykv[...] = jnp.zeros_like(ykv)

    @pl.when(jnp.logical_not(has_other))
    def _():
        co[...] = jnp.zeros_like(co)

    pl.semaphore_wait(barrier, jnp.where(has_n, 3, 1))

    @pl.when(has_n)
    def _():
        for copy in keys + tri[::-1]:
            copy.start()

    for d in (dm, do):
        for k in range(3):
            d[k, (k + 1) * B:, :] = jnp.zeros((SUPER - (k + 1) * B, B), BF)
            d[9 + k, : (k + 1) * B, :] = jnp.zeros(((k + 1) * B, B), BF)
    for s in range(1, 4):
        k = jnp.where(l == 1, s - 1, 4 - s)
        start = pl.multiple_of(jnp.where(l == 1, s * B, 0), B)
        rnm[k, pl.ds(start, (4 - s) * B), :] = jnp.zeros(((4 - s) * B, B), BF)

    def mask(ref, k, i, keep):
        rows = pl.ds(i * B if isinstance(i, int) else pl.multiple_of(i * B, B), B)
        ref[k, rows, :] = ref[k, rows, :] * jnp.full((B, B), keep.astype(F32), F32).astype(BF)

    def mask_rows(srow, d):
        for i in range(4):
            for g in range(WIDTH):
                mask(d, g + i, i, xk[4 * srow + i, g])

    for copy in keeps + loads[:4]:
        copy.wait()
    mask_rows(l, dm)
    for copy in loads[4:]:
        copy.wait()
    mask_rows(1 - l, do)

    def cat(ref, base=0, count=4, rows=slice(None)):
        return jnp.concatenate([ref[base + j, rows, :] for j in range(count)], axis=1)

    def lhs(*pieces):
        return jnp.concatenate([cat(*p) for p in pieces], axis=1)

    def rhs(*pieces):
        return jnp.concatenate([cat(*p) for p in pieces], axis=0)

    def dot(a, b):
        return jnp.dot(a, b, preferred_element_type=F32)

    def put(ref, value):
        for j in range(value.shape[1] // B):
            ref[j] = value[:, j * B:(j + 1) * B]

    def store_y(dst, value, table, first, h, base=0, col=0, row=0):
        for i in range(row, row + value.shape[0] // B):
            for j in range(value.shape[1] // B):
                keep = table[first + i, jnp.clip(h + col + j - i, 0, 4 * W)].astype(F32) * scale
                block = value[(i - row) * B:(i - row + 1) * B, j * B:(j + 1) * B]
                dst[base + j, i * B:(i + 1) * B, :] = (block * keep).astype(BF)

    def to_sib(src, dst, index):
        return pltpu.make_async_remote_copy(src, dst, y_s.at[index], y_r.at[index], device_id=sib, device_id_type=MESH)

    send_ymo, send_ymp, send_ymm = to_sib(ymo, yom, 0), to_sib(ymp, yon, 1), to_sib(ymm, yoo, 2)
    mo, mm, mn = (dm, b_mo), (dm, 4), (dm, b_mn)
    theirs = 4 * (1 - l)
    z_out, c_out = NC * l, NZ * (1 - l)
    z_in, c_in = NC * (1 - l), NZ * l
    send_z = pltpu.make_async_remote_copy(zs, zr, z_s, z_r, device_id=facing, device_id_type=MESH)

    put(acc_mm, dot(lhs(mo, mm), rhs((do, b_om), mm)))
    zs[...] = acc_mm[z_out].astype(BF)
    store_y(ymo, dot(lhs(mo, mm), rhs((do, 4), mo)), yk, 4 * l, 12 - 8 * l)
    send_ymo.start()
    store_y(ymp, dot(cat(*mo), cat(do, b_op)), yk, 4 * l, 16 - 16 * l)
    send_ymp.start()

    @pl.when(jnp.logical_and(has_n, jnp.logical_not(early)))
    def _():
        tri[1].wait_send()
        for copy in mid:
            copy.start()

    @pl.when(has_n)
    def _():
        for copy in keys:
            copy.wait()

    to_smem = [pltpu.make_async_copy(xkv, xkn, k_sem.at[0]), pltpu.make_async_copy(ykv, ykn, k_sem.at[1])]
    for copy in to_smem:
        copy.start()
    put(acc_ymn, dot(cat(*mm), cat(*mn)))
    for copy in to_smem:
        copy.wait()


    put(acc_mo, dot(cat(*mm), cat(ymo)))
    send_ymo.wait_recv()
    put(acc_o, dot(cat(*mo), cat(yom)))
    send_ymp.wait_recv()
    put(acc_mn, dot(cat(*mo), cat(yon)))

    @pl.when(early)
    def _():
        tri[1].wait_send()
        for copy in mid:
            copy.start()

    @pl.when(late)
    def _():
        for copy in mid:
            copy.wait_send()

    @pl.when(has_n)
    def _():
        send_z.start()

    def mask_tri(q):
        i, e = side(l == 0, q)
        for t in range(q + 1):
            mask(rnm, jnp.where(l == 0, 0, i) + t, i, xkn[theirs + i, e + t])

    @pl.when(has_n)
    def _():
        for copy in tri:
            copy.wait_recv()

    for q in range(4):
        mask_tri(q)
    part = pl.ds(pl.multiple_of(c_out * B, B), NC * B)
    value = cat(acc_mm, c_out, NC) + dot(cat(dm, b_mn + c_out, NC), cat(rnm, c_out, NC, part))
    store_y(ymm, value, yk, 4 * l, 8, c_out, c_out)
    c = dot(cat(rnm, 0, 4, part), cat(ymm, c_out, NC))

    def pick(value, first, a, b):
        block = value[a * B:(a + 1) * B, b * B:(b + 1) * B]
        return block if a == b else jnp.where(first, block, value[b * B:(b + 1) * B, a * B:(a + 1) * B])

    for n, (a, b) in enumerate(PAIRS[:NP]):
        block = pick(c, l == 0, a, b).astype(BF)
        for h in range(2):
            cs[h, n] = block[h * HALF:(h + 1) * HALF]
    c_facing, c_same = [
        pltpu.make_async_remote_copy(cs.at[h], dst, c_s.at[n], c_r.at[n], device_id=there, device_id_type=MESH)
        for n, (h, dst, there) in enumerate(((1 - l, cm, facing), (l, co, same)))
    ]

    @pl.when(has_n)
    def _():
        c_facing.start()
        c_same.start()

    store_y(ymm, acc_mm[z_out] + dot(cat(*mn), rnm[z_out]), yk, 4 * l, 8, z_out, z_out)
    send_ymm.start()
    store_y(yno, dot(cat(rnm), cat(*mo)), ykn, theirs, 16 - 16 * l)
    put(acc_ynm, dot(cat(rnm), cat(*mm)))
    acc_z[...] = dot(cat(rnm), dm[b_mn + z_in])

    def finish(cube, base, i, j):
        keep = xk[4 * l + i, base + j - i].astype(F32)
        rows = pl.ds(i * B if isinstance(i, int) else pl.multiple_of(i * B, B), B)
        own = dm[base + j, rows, :].astype(F32)
        return ((1.5 * own - (0.5 * scale) * cube) * keep).astype(BF)

    def stage(cube, base, i, j):
        block = finish(cube, base, i, j)
        low, high = block[:HALF], block[HALF:]
        out_ref[4 * l + i, base + j - i] = jnp.where(l == 0, low, high)
        stg[i, base + j - i] = jnp.where(l == 0, high, low)

    def outs(n, i, e, count):
        return pltpu.make_async_remote_copy(
            stg.at[i, pl.ds(e, count)], out_ref.at[4 * l + i, pl.ds(e, count)], o_s.at[n], o_r.at[n],
            device_id=sib, device_id_type=MESH)

    put(acc_o, cat(acc_o) + dot(cat(*mm), cat(ymm)))
    send_ymm.wait_recv()
    value = cat(acc_mo) + dot(lhs(mo, mn), rhs((yoo,), (yno,)))
    for a, b in PAIRS:
        stage(pick(value, l == 0, a, b), b_mo, jnp.where(l == 0, a, b), jnp.where(l == 0, b, a))
    out_a = []
    for q in range(4):
        i, e = side(l == 0, q)
        out_a.append(outs(q, i, e, q + 1))
    for copy in out_a:
        copy.start()

    for first in (0, 2):
        rows = slice(first * B, (first + 2) * B)

        @pl.when(has_n)
        def _(first=first):
            for copy in mid[first:first + 2]:
                copy.wait_recv()

        for i in range(first, first + 2):
            for j in range(4):
                mask(rnn, j, i, xkn[theirs + i, 4 + j - i])
        part = cat(dm, b_mn + first, 2)
        value = cat(acc_ymn) + dot(part, cat(rnn, 0, 4, rows))
        if first == 0:
            put(acc_ymn, value)
        else:
            store_y(ymn, value, yk, 4 * l, 4 + 8 * l)
            c_rows = pl.ds(pl.multiple_of(c_in * B, B), NC * B)
            value = cat(acc_mn, c_in, NC, c_rows) + dot(cat(dm, 4, 4, c_rows), cat(ymn, c_in, NC))
            for n, (a, b) in enumerate(PAIRS[:NP]):
                i, j = jnp.where(l == 1, NZ + a, b), jnp.where(l == 1, NZ + b, a)
                block = finish(pick(value, l == 1, a, b), b_mn, i, j)
                for h in range(2):
                    pb[h, n] = block[h * HALF:(h + 1) * HALF]
            send_p = pltpu.make_async_remote_copy(pb.at[1 - l], po, p_s, p_r, device_id=sib, device_id_type=MESH)
            send_p.start()
        value = cat(acc_ynm, 0, 4, rows) + dot(cat(rnn, 0, 4, rows), cat(rnm))
        store_y(ynm, value, ykn, theirs, 12 - 8 * l, row=first)
        value = cat(acc_o) + dot(part, cat(ynm, 0, 4, rows))
        if first == 0:
            put(acc_o, value)
    out_m = []
    for i in range(4):
        for j in range(4):
            stage(value[i * B:(i + 1) * B, j * B:(j + 1) * B], 4, i, j)
        out_m.append(outs(4 + i, i, 4 - i, 4))
        out_m[i].start()
    value = acc_mn[z_in] + dot(cat(*mm), ymn[z_in])

    @pl.when(has_n)
    def _():
        send_z.wait_recv()

    store_y(yz, zr[...].astype(F32) + acc_z[...], ykn, theirs, 8, 0, z_in)
    value = value + dot(cat(*mn), yz[0])
    out_z = []
    for i in range(4):
        stage(value[i * B:(i + 1) * B], b_mn, i, z_in)
        out_z.append(outs(8 + i, i, b_mn + z_in - i, 1))
        out_z[i].start()

    send_p.wait_recv()

    def add(srow, part, term):
        for n, (a, b) in enumerate(PAIRS[:NP]):
            i = jnp.where(srow == 1, NZ + a, b)
            e = jnp.where(srow == 1, 2 * W + b - a, a - b)
            keep = xk[4 * srow + i, e].astype(F32) * (0.5 * scale)
            out_ref[4 * srow + i, e] = (part[n].astype(F32) - keep * term[n].astype(F32)).astype(BF)

    @pl.when(has_n)
    def _():
        c_facing.wait_recv()

    add(l, pb.at[l], cm)

    @pl.when(has_other)
    def _():
        c_same.wait_recv()

    add(1 - l, po, co)

    for copy in out_a + out_m + out_z:
        copy.wait()
    for copy in (send_ymo, send_ymp, send_ymm, send_p):
        copy.wait_send()

    @pl.when(has_n)
    def _():
        for copy in tri[:1] + tri[2:] + [send_z, c_facing, c_same]:
            copy.wait_send()

    @pl.when(jnp.logical_and(has_n, jnp.logical_not(late)))
    def _():
        for copy in mid:
            copy.wait_send()


def solution(mesh):
    cols = mesh.shape["col"]
    groups = mesh.shape["row"] * cols

    def step(xband, xkeep, ykeep):
        scale = (2.0 * WIDTH * B) ** -0.5
        rows = xband.shape[0]
        dense = lambda n, dtype=BF: pltpu.VMEM((n, SUPER, B), dtype)
        sems = lambda *n: pltpu.SemaphoreType.DMA(n)
        halves = lambda *n: pltpu.VMEM((*n, HALF, B), BF)
        scratch = (
            [dense(12), dense(12)] + [dense(4)] * 11 + [dense(4, F32)] * 6
            + [pltpu.VMEM((SUPER, B), F32), pltpu.VMEM((SUPER, B), BF), pltpu.VMEM((SUPER, B), BF), dense(1)]
            + [halves(2, NP), halves(NP), halves(NP), halves(4, WIDTH), halves(2, NP), halves(NP)]
            + [pltpu.SMEM(a.shape, jnp.int32) for a in (xkeep, ykeep, xkeep, ykeep)]
            + [pltpu.VMEM(a.shape, jnp.int32) for a in (xkeep, ykeep)]
            + [sems(2, 4), sems(2), sems(4), sems(4), sems(4), sems(4), sems(2), sems(2), sems(3), sems(3)]
            + [sems(), sems(), sems(2), sems(2), sems(12), sems(12), sems(), sems()]
        )
        args = [pltpu.with_memory_space_constraint(a, pltpu.HBM) for a in (xband, xkeep, ykeep)]
        return pl.pallas_call(
            functools.partial(kernel, groups, cols, scale),
            out_shape=jax.ShapeDtypeStruct((rows, WIDTH, HALF, B), BF),
            in_specs=[pl.BlockSpec(memory_space=pl.ANY)] * 3,
            out_specs=pl.BlockSpec(memory_space=pltpu.VMEM),
            scratch_shapes=scratch,
            compiler_params=pltpu.CompilerParams(
                collective_id=0, has_side_effects=True, vmem_limit_bytes=40 * 2**20),
        )(*args)

    in_specs = (P(("row", "col"), None, None, None), P(("row", "col"), None), P(("row", "col"), None))
    return jax.shard_map(step, mesh=mesh, in_specs=in_specs, out_specs=P(("row", "col"), None, "layer", None), check_vma=False)
```

```python
import functools

import jax
import jax.numpy as jnp
from jax import lax
from jax.experimental import pallas as pl
from jax.experimental.pallas import tpu as pltpu
from jax.sharding import PartitionSpec as P

B = 128
W = 4
LAST = 7
NC = 3
NZ = W - NC
PAIRS = [(a, b) for a in range(W) for b in range(a + 1)]
NP = NC * (NC + 1) // 2
WIDTH = 2 * W + 1
SUPER = W * B
HALF = B // 2
MESH = pl.DeviceIdType.MESH
BF = jnp.bfloat16
F32 = jnp.float32


def kernel(
    groups, cols, scale,
    x_hbm, xk_hbm, yk_hbm, out_ref,
    dm, do, rnm, rnn, ymo, ymm, ymp, yom, yoo, yon, ynm, yno, ymn,
    acc_mm, acc_mn, acc_o, acc_mo, acc_ynm, acc_ymn, acc_z, zs, zr, yz, cs, cm, co, fw, stg, pb, po, xk, yk, xkn, ykn, xkv, ykv,
    in_sem, k_sem, tri_s, tri_r, mid_s, mid_r, key_s, key_r, y_s, y_r, z_s, z_r, c_s, c_r,
    o_s, o_r, p_s, p_r,
):
    row, col, l = lax.axis_index("row"), lax.axis_index("col"), lax.axis_index("layer")
    group = row * cols + col
    step = 2 * l - 1

    def device(g, layer):
        g = lax.rem(g + groups, groups)
        return (g // cols, lax.rem(g, cols), layer)

    sib = (row, col, 1 - l)
    facing = device(group + step, 1 - l)
    same = device(group + step, l)
    other = device(group - step, l)
    has_n = jnp.logical_and(group + step >= 0, group + step < groups)
    has_other = jnp.logical_and(group - step >= 0, group - step < groups)

    early = jnp.logical_and(has_n, jnp.logical_and(l == 0, lax.rem(col, LAST + 1) == 0))
    beside_late = jnp.logical_and(l == 0, lax.rem(col, LAST + 1) == LAST)
    late = jnp.logical_and(has_n, jnp.logical_and(l == 1, lax.rem(col, LAST + 1) == LAST))

    barrier = pltpu.get_barrier_semaphore()
    pl.semaphore_signal(barrier, inc=1, device_id=sib, device_id_type=MESH)

    @pl.when(has_n)
    def _():
        pl.semaphore_signal(barrier, inc=1, device_id=facing, device_id_type=MESH)

    @pl.when(jnp.logical_and(has_other, jnp.logical_not(beside_late)))
    def _():
        pl.semaphore_signal(barrier, inc=1, device_id=other, device_id_type=MESH)

    b_mo, b_mn, b_om, b_op = 8 * (1 - l), 8 * l, 8 * l, 8 * (1 - l)

    def side(right, q):
        return jnp.where(right, q, 3 - q), jnp.where(right, 8 - q, 0)

    keeps = [pltpu.make_async_copy(xk_hbm, xk, k_sem.at[0]), pltpu.make_async_copy(yk_hbm, yk, k_sem.at[1])]
    loads = [
        pltpu.make_async_copy(x_hbm.at[4 * s + i], d.at[pl.ds(i, WIDTH), pl.ds(i * B, B)], in_sem.at[n, i])
        for n, (s, d) in enumerate(((l, dm), (1 - l, do)))
        for i in range(4)
    ]
    @pl.when(jnp.logical_not(late))
    def _():
        for copy in keeps + loads:
            copy.start()

    keys = [
        pltpu.make_async_remote_copy(src, dst, key_s.at[n], key_r.at[n], device_id=facing, device_id_type=MESH)
        for n, (src, dst) in enumerate(((xk_hbm, xkv), (yk_hbm, ykv)))
    ]
    tri, mid = [], []
    for q in range(4):
        i, e = side(l == 1, q)
        rows = pl.ds(pl.multiple_of(i * B, B), B)
        tri.append(pltpu.make_async_remote_copy(
            x_hbm.at[4 * l + i, pl.ds(e, q + 1)], rnm.at[pl.ds(jnp.where(l == 1, 0, i), q + 1), rows],
            tri_s.at[q], tri_r.at[q], device_id=facing, device_id_type=MESH))
    for i in range(4):
        mid.append(pltpu.make_async_remote_copy(
            x_hbm.at[4 * l + i, pl.ds(4 - i, 4)], rnn.at[:, pl.ds(i * B, B)],
            mid_s.at[i], mid_r.at[i], device_id=facing, device_id_type=MESH))

    @pl.when(jnp.logical_not(has_n))
    def _():
        rnm[...] = jnp.zeros_like(rnm)
        rnn[...] = jnp.zeros_like(rnn)
        zr[...] = jnp.zeros_like(zr)
        cm[...] = jnp.zeros_like(cm)
        xkv[...] = jnp.zeros_like(xkv)
        ykv[...] = jnp.zeros_like(ykv)

    @pl.when(jnp.logical_not(has_other))
    def _():
        co[...] = jnp.zeros_like(co)

    pl.semaphore_wait(barrier, jnp.where(has_n, jnp.where(early, 2, 3), 1))

    @pl.when(has_n)
    def _():
        for copy in keys + tri[::-1]:
            copy.start()

    @pl.when(late)
    def _():
        for copy in keeps + loads:
            copy.start()

    for d in (dm, do):
        for k in range(3):
            d[k, (k + 1) * B:, :] = jnp.zeros((SUPER - (k + 1) * B, B), BF)
            d[9 + k, : (k + 1) * B, :] = jnp.zeros(((k + 1) * B, B), BF)
    for s in range(1, 4):
        k = jnp.where(l == 1, s - 1, 4 - s)
        start = pl.multiple_of(jnp.where(l == 1, s * B, 0), B)
        rnm[k, pl.ds(start, (4 - s) * B), :] = jnp.zeros(((4 - s) * B, B), BF)

    def mask(ref, k, i, keep):
        rows = pl.ds(i * B if isinstance(i, int) else pl.multiple_of(i * B, B), B)
        ref[k, rows, :] = ref[k, rows, :] * jnp.full((B, B), keep.astype(F32), F32).astype(BF)

    def mask_rows(srow, d):
        for i in range(4):
            for g in range(WIDTH):
                mask(d, g + i, i, xk[4 * srow + i, g])

    for copy in keeps + loads[:4]:
        copy.wait()
    mask_rows(l, dm)
    for copy in loads[4:]:
        copy.wait()
    mask_rows(1 - l, do)

    def cat(ref, base=0, count=4, rows=slice(None)):
        return jnp.concatenate([ref[base + j, rows, :] for j in range(count)], axis=1)

    def lhs(*pieces):
        return jnp.concatenate([cat(*p) for p in pieces], axis=1)

    def rhs(*pieces):
        return jnp.concatenate([cat(*p) for p in pieces], axis=0)

    def dot(a, b):
        return jnp.dot(a, b, preferred_element_type=F32)

    def put(ref, value):
        for j in range(value.shape[1] // B):
            ref[j] = value[:, j * B:(j + 1) * B]

    def store_y(dst, value, table, first, h, base=0, col=0, row=0):
        for i in range(row, row + value.shape[0] // B):
            for j in range(value.shape[1] // B):
                keep = table[first + i, jnp.clip(h + col + j - i, 0, 4 * W)].astype(F32) * scale
                block = value[(i - row) * B:(i - row + 1) * B, j * B:(j + 1) * B]
                dst[base + j, i * B:(i + 1) * B, :] = (block * keep).astype(BF)

    def to_sib(src, dst, index):
        return pltpu.make_async_remote_copy(src, dst, y_s.at[index], y_r.at[index], device_id=sib, device_id_type=MESH)

    send_ymo, send_ymp, send_ymm = to_sib(ymo, yom, 0), to_sib(ymp, yon, 1), to_sib(ymm, yoo, 2)
    mo, mm, mn = (dm, b_mo), (dm, 4), (dm, b_mn)
    theirs = 4 * (1 - l)
    z_out, c_out = NC * l, NZ * (1 - l)
    z_in, c_in = NC * (1 - l), NZ * l
    send_z = pltpu.make_async_remote_copy(zs, zr, z_s, z_r, device_id=facing, device_id_type=MESH)

    put(acc_mm, dot(lhs(mo, mm), rhs((do, b_om), mm)))
    zs[...] = acc_mm[z_out].astype(BF)
    store_y(ymo, dot(lhs(mo, mm), rhs((do, 4), mo)), yk, 4 * l, 12 - 8 * l)
    send_ymo.start()
    store_y(ymp, dot(cat(*mo), cat(do, b_op)), yk, 4 * l, 16 - 16 * l)
    send_ymp.start()

    @pl.when(jnp.logical_and(has_n, jnp.logical_not(early)))
    def _():
        tri[1].wait_send()
        for copy in mid[:2]:
            copy.start()

    @pl.when(jnp.logical_and(has_n, jnp.logical_not(jnp.logical_or(early, late))))
    def _():
        for copy in mid[2:]:
            copy.start()

    put(acc_ymn, dot(cat(*mm), cat(*mn)))

    put(acc_mo, dot(cat(*mm), cat(ymo)))
    send_ymo.wait_recv()
    put(acc_o, dot(cat(*mo), cat(yom)))
    send_ymp.wait_recv()
    put(acc_mn, dot(cat(*mo), cat(yon)))

    @pl.when(early)
    def _():
        tri[1].wait_send()
        for copy in mid[:2]:
            copy.start()

    @pl.when(jnp.logical_or(early, late))
    def _():
        for copy in mid[2:]:
            copy.start()

    @pl.when(has_n)
    def _():
        for copy in keys:
            copy.wait()

    to_smem = [pltpu.make_async_copy(xkv, xkn, k_sem.at[0]), pltpu.make_async_copy(ykv, ykn, k_sem.at[1])]
    for copy in to_smem:
        copy.start()
    for copy in to_smem:
        copy.wait()

    @pl.when(has_n)
    def _():
        send_z.start()

    def mask_tri(q):
        i, e = side(l == 0, q)
        for t in range(q + 1):
            mask(rnm, jnp.where(l == 0, 0, i) + t, i, xkn[theirs + i, e + t])

    @pl.when(has_n)
    def _():
        for copy in tri[1:]:
            copy.wait_recv()

    for q in range(1, 4):
        mask_tri(q)
    part = pl.ds(pl.multiple_of(c_out * B, B), NC * B)
    value = cat(acc_mm, c_out, NC) + dot(cat(dm, b_mn + c_out, NC), cat(rnm, c_out, NC, part))
    store_y(ymm, value, yk, 4 * l, 8, c_out, c_out)
    c = dot(cat(rnm, 0, 4, part), cat(ymm, c_out, NC))

    def pick(value, first, a, b):
        block = value[a * B:(a + 1) * B, b * B:(b + 1) * B]
        return block if a == b else jnp.where(first, block, value[b * B:(b + 1) * B, a * B:(a + 1) * B])

    for n, (a, b) in enumerate(PAIRS[:NP]):
        block = pick(c, l == 0, a, b).astype(BF)
        for h in range(2):
            cs[h, n] = block[h * HALF:(h + 1) * HALF]
    def send_c(src, dst, send, recv, there):
        return pltpu.make_async_remote_copy(src, dst, c_s.at[send], c_r.at[recv], device_id=there, device_id_type=MESH)

    c_facing = send_c(cs.at[1 - l], cm, 0, 0, facing)
    c_same = send_c(cs.at[l], co, 1, 1, same)
    c_late = send_c(cs.at[l], fw, 2, 2, facing)
    c_forward = send_c(fw, co, 3, 1, sib)

    @pl.when(jnp.logical_and(has_n, jnp.logical_not(early)))
    def _():
        c_same.start()

    @pl.when(early)
    def _():
        c_late.start()

    @pl.when(has_n)
    def _():
        c_facing.start()

    @pl.when(has_n)
    def _():
        tri[0].wait_recv()

    mask_tri(0)
    store_y(ymm, acc_mm[z_out] + dot(cat(*mn), rnm[z_out]), yk, 4 * l, 8, z_out, z_out)
    send_ymm.start()
    store_y(yno, dot(cat(rnm), cat(*mo)), ykn, theirs, 16 - 16 * l)
    put(acc_ynm, dot(cat(rnm), cat(*mm)))
    acc_z[...] = dot(cat(rnm), dm[b_mn + z_in])

    def finish(cube, base, i, j):
        keep = xk[4 * l + i, base + j - i].astype(F32)
        rows = pl.ds(i * B if isinstance(i, int) else pl.multiple_of(i * B, B), B)
        own = dm[base + j, rows, :].astype(F32)
        return ((1.5 * own - (0.5 * scale) * cube) * keep).astype(BF)

    def stage(cube, base, i, j):
        block = finish(cube, base, i, j)
        low, high = block[:HALF], block[HALF:]
        out_ref[4 * l + i, base + j - i] = jnp.where(l == 0, low, high)
        stg[i, base + j - i] = jnp.where(l == 0, high, low)

    def outs(n, i, e, count):
        return pltpu.make_async_remote_copy(
            stg.at[i, pl.ds(e, count)], out_ref.at[4 * l + i, pl.ds(e, count)], o_s.at[n], o_r.at[n],
            device_id=sib, device_id_type=MESH)

    put(acc_o, cat(acc_o) + dot(cat(*mm), cat(ymm)))
    send_ymm.wait_recv()
    value = cat(acc_mo) + dot(lhs(mo, mn), rhs((yoo,), (yno,)))
    for a, b in PAIRS:
        stage(pick(value, l == 0, a, b), b_mo, jnp.where(l == 0, a, b), jnp.where(l == 0, b, a))
    out_a = []
    for q in range(4):
        i, e = side(l == 0, q)
        out_a.append(outs(q, i, e, q + 1))
    for copy in out_a:
        copy.start()

    for first in (0, 2):
        rows = slice(first * B, (first + 2) * B)

        @pl.when(has_n)
        def _(first=first):
            for copy in mid[first:first + 2]:
                copy.wait_recv()

        for i in range(first, first + 2):
            for j in range(4):
                mask(rnn, j, i, xkn[theirs + i, 4 + j - i])
        part = cat(dm, b_mn + first, 2)
        value = cat(acc_ynm, 0, 4, rows) + dot(cat(rnn, 0, 4, rows), cat(rnm))
        store_y(ynm, value, ykn, theirs, 12 - 8 * l, row=first)
        value = cat(acc_o) + dot(part, cat(ynm, 0, 4, rows))
        if first == 0:
            put(acc_o, value)
            put(acc_ymn, cat(acc_ymn) + dot(part, cat(rnn, 0, 4, rows)))
    store_y(ymn, cat(acc_ymn) + dot(part, cat(rnn, 0, 4, rows)), yk, 4 * l, 4 + 8 * l)
    c_rows = pl.ds(pl.multiple_of(c_in * B, B), NC * B)
    part_c = cat(acc_mn, c_in, NC, c_rows) + dot(cat(dm, 4, 4, c_rows), cat(ymn, c_in, NC))
    for n, (a, b) in enumerate(PAIRS[:NP]):
        i, j = jnp.where(l == 1, NZ + a, b), jnp.where(l == 1, NZ + b, a)
        block = finish(pick(part_c, l == 1, a, b), b_mn, i, j)
        for h in range(2):
            pb[h, n] = block[h * HALF:(h + 1) * HALF]
    send_p = pltpu.make_async_remote_copy(pb.at[1 - l], po, p_s, p_r, device_id=sib, device_id_type=MESH)
    send_p.start()
    out_m = []
    for i in range(4):
        for j in range(4):
            stage(value[i * B:(i + 1) * B, j * B:(j + 1) * B], 4, i, j)
        out_m.append(outs(4 + i, i, 4 - i, 4))
        out_m[i].start()
    value = acc_mn[z_in] + dot(cat(*mm), ymn[z_in])

    @pl.when(has_n)
    def _():
        send_z.wait_recv()

    store_y(yz, zr[...].astype(F32) + acc_z[...], ykn, theirs, 8, 0, z_in)
    value = value + dot(cat(*mn), yz[0])
    out_z = []
    for i in range(4):
        stage(value[i * B:(i + 1) * B], b_mn, i, z_in)
        out_z.append(outs(8 + i, i, b_mn + z_in - i, 1))
        out_z[i].start()

    send_p.wait_recv()

    def add(srow, part, term):
        for n, (a, b) in enumerate(PAIRS[:NP]):
            i = jnp.where(srow == 1, NZ + a, b)
            e = jnp.where(srow == 1, 2 * W + b - a, a - b)
            keep = xk[4 * srow + i, e].astype(F32) * (0.5 * scale)
            out_ref[4 * srow + i, e] = (part[n].astype(F32) - keep * term[n].astype(F32)).astype(BF)

    @pl.when(late)
    def _():
        c_late.wait_recv()
        c_forward.start()

    @pl.when(has_n)
    def _():
        c_facing.wait_recv()

    add(l, pb.at[l], cm)

    @pl.when(has_other)
    def _():
        c_same.wait_recv()

    add(1 - l, po, co)

    for copy in out_a + out_m + out_z:
        copy.wait()
    for copy in (send_ymo, send_ymp, send_ymm, send_p):
        copy.wait_send()

    @pl.when(has_n)
    def _():
        for copy in tri[:1] + tri[2:] + [send_z, c_facing]:
            copy.wait_send()

    @pl.when(early)
    def _():
        c_late.wait_send()

    @pl.when(jnp.logical_and(has_n, jnp.logical_not(early)))
    def _():
        c_same.wait_send()

    @pl.when(late)
    def _():
        c_forward.wait_send()

    @pl.when(has_n)
    def _():
        for copy in mid:
            copy.wait_send()


def solution(mesh):
    cols = mesh.shape["col"]
    groups = mesh.shape["row"] * cols

    def step(xband, xkeep, ykeep):
        scale = (2.0 * WIDTH * B) ** -0.5
        rows = xband.shape[0]
        dense = lambda n, dtype=BF: pltpu.VMEM((n, SUPER, B), dtype)
        sems = lambda *n: pltpu.SemaphoreType.DMA(n)
        halves = lambda *n: pltpu.VMEM((*n, HALF, B), BF)
        scratch = (
            [dense(12), dense(12)] + [dense(4)] * 11 + [dense(4, F32)] * 6
            + [pltpu.VMEM((SUPER, B), F32), pltpu.VMEM((SUPER, B), BF), pltpu.VMEM((SUPER, B), BF), dense(1)]
            + [halves(2, NP), halves(NP), halves(NP), halves(NP), halves(4, WIDTH), halves(2, NP), halves(NP)]
            + [pltpu.SMEM(a.shape, jnp.int32) for a in (xkeep, ykeep, xkeep, ykeep)]
            + [pltpu.VMEM(a.shape, jnp.int32) for a in (xkeep, ykeep)]
            + [sems(2, 4), sems(2), sems(4), sems(4), sems(4), sems(4), sems(2), sems(2), sems(3), sems(3)]
            + [sems(), sems(), sems(4), sems(3), sems(12), sems(12), sems(), sems()]
        )
        args = [pltpu.with_memory_space_constraint(a, pltpu.HBM) for a in (xband, xkeep, ykeep)]
        return pl.pallas_call(
            functools.partial(kernel, groups, cols, scale),
            out_shape=jax.ShapeDtypeStruct((rows, WIDTH, HALF, B), BF),
            in_specs=[pl.BlockSpec(memory_space=pl.ANY)] * 3,
            out_specs=pl.BlockSpec(memory_space=pltpu.VMEM),
            scratch_shapes=scratch,
            compiler_params=pltpu.CompilerParams(
                collective_id=0, has_side_effects=True, vmem_limit_bytes=40 * 2**20),
        )(*args)

    in_specs = (P(("row", "col"), None, None, None), P(("row", "col"), None), P(("row", "col"), None))
    return jax.shard_map(step, mesh=mesh, in_specs=in_specs, out_specs=P(("row", "col"), None, "layer", None), check_vma=False)
```

```python
import functools

import jax
import jax.numpy as jnp
from jax import lax
from jax.experimental import pallas as pl
from jax.experimental.pallas import tpu as pltpu
from jax.sharding import PartitionSpec as P

B = 128
W = 4
LAST = 7
NC = 3
NZ = W - NC
PAIRS = [(a, b) for a in range(W) for b in range(a + 1)]
NP = NC * (NC + 1) // 2
WIDTH = 2 * W + 1
SUPER = W * B
HALF = B // 2
MESH = pl.DeviceIdType.MESH
BF = jnp.bfloat16
F32 = jnp.float32


def kernel(
    groups, cols, scale,
    x_hbm, xk_hbm, yk_hbm, out_ref,
    dm, do, rnm, rnn, ymo, ymm, ymp, yom, yoo, yon, ynm, yno, ymn,
    acc_mm, acc_mn, acc_o, acc_mo, acc_ynm, acc_ymn, acc_z, zs, zr, yz, cs, cm, co, fw, stg, pb, po, xk, yk, xkn, ykn, xkv, ykv,
    in_sem, k_sem, tri_s, tri_r, mid_s, mid_r, key_s, key_r, y_s, y_r, z_s, z_r, c_s, c_r,
    o_s, o_r, p_s, p_r,
):
    row, col, l = lax.axis_index("row"), lax.axis_index("col"), lax.axis_index("layer")
    group = row * cols + col
    step = 2 * l - 1

    def device(g, layer):
        g = lax.rem(g + groups, groups)
        return (g // cols, lax.rem(g, cols), layer)

    sib = (row, col, 1 - l)
    facing = device(group + step, 1 - l)
    same = device(group + step, l)
    other = device(group - step, l)
    has_n = jnp.logical_and(group + step >= 0, group + step < groups)
    has_other = jnp.logical_and(group - step >= 0, group - step < groups)

    early = jnp.logical_and(has_n, jnp.logical_and(l == 0, lax.rem(col, LAST + 1) == 0))
    beside_late = jnp.logical_and(l == 0, lax.rem(col, LAST + 1) == LAST)
    late = jnp.logical_and(has_n, jnp.logical_and(l == 1, lax.rem(col, LAST + 1) == LAST))

    barrier = pltpu.get_barrier_semaphore()
    pl.semaphore_signal(barrier, inc=1, device_id=sib, device_id_type=MESH)

    @pl.when(has_n)
    def _():
        pl.semaphore_signal(barrier, inc=1, device_id=facing, device_id_type=MESH)

    @pl.when(jnp.logical_and(has_other, jnp.logical_not(beside_late)))
    def _():
        pl.semaphore_signal(barrier, inc=1, device_id=other, device_id_type=MESH)

    b_mo, b_mn, b_om, b_op = 8 * (1 - l), 8 * l, 8 * l, 8 * (1 - l)

    def side(right, q):
        return jnp.where(right, q, 3 - q), jnp.where(right, 8 - q, 0)

    keeps = [pltpu.make_async_copy(xk_hbm, xk, k_sem.at[0]), pltpu.make_async_copy(yk_hbm, yk, k_sem.at[1])]
    loads = [
        pltpu.make_async_copy(x_hbm.at[4 * s + i], d.at[pl.ds(i, WIDTH), pl.ds(i * B, B)], in_sem.at[n, i])
        for n, (s, d) in enumerate(((l, dm), (1 - l, do)))
        for i in range(4)
    ]
    @pl.when(jnp.logical_not(late))
    def _():
        for copy in keeps + loads:
            copy.start()

    keys = [
        pltpu.make_async_remote_copy(src, dst, key_s.at[n], key_r.at[n], device_id=facing, device_id_type=MESH)
        for n, (src, dst) in enumerate(((xk_hbm, xkv), (yk_hbm, ykv)))
    ]
    tri, mid = [], []
    for q in range(4):
        i, e = side(l == 1, q)
        rows = pl.ds(pl.multiple_of(i * B, B), B)
        tri.append(pltpu.make_async_remote_copy(
            x_hbm.at[4 * l + i, pl.ds(e, q + 1)], rnm.at[pl.ds(jnp.where(l == 1, 0, i), q + 1), rows],
            tri_s.at[q], tri_r.at[q], device_id=facing, device_id_type=MESH))
    for i in range(4):
        mid.append(pltpu.make_async_remote_copy(
            x_hbm.at[4 * l + i, pl.ds(4 - i, 4)], rnn.at[:, pl.ds(i * B, B)],
            mid_s.at[i], mid_r.at[i], device_id=facing, device_id_type=MESH))

    @pl.when(jnp.logical_not(has_n))
    def _():
        rnm[...] = jnp.zeros_like(rnm)
        rnn[...] = jnp.zeros_like(rnn)
        zr[...] = jnp.zeros_like(zr)
        cm[...] = jnp.zeros_like(cm)
        xkv[...] = jnp.zeros_like(xkv)
        ykv[...] = jnp.zeros_like(ykv)

    @pl.when(jnp.logical_not(has_other))
    def _():
        co[...] = jnp.zeros_like(co)

    pl.semaphore_wait(barrier, jnp.where(has_n, jnp.where(early, 2, 3), 1))

    @pl.when(has_n)
    def _():
        for copy in keys + tri[::-1] + mid:
            copy.start()

    @pl.when(late)
    def _():
        for copy in keeps + loads:
            copy.start()

    for d in (dm, do):
        for k in range(3):
            d[k, (k + 1) * B:, :] = jnp.zeros((SUPER - (k + 1) * B, B), BF)
            d[9 + k, : (k + 1) * B, :] = jnp.zeros(((k + 1) * B, B), BF)
    for s in range(1, 4):
        k = jnp.where(l == 1, s - 1, 4 - s)
        start = pl.multiple_of(jnp.where(l == 1, s * B, 0), B)
        rnm[k, pl.ds(start, (4 - s) * B), :] = jnp.zeros(((4 - s) * B, B), BF)

    def mask(ref, k, i, keep):
        rows = pl.ds(i * B if isinstance(i, int) else pl.multiple_of(i * B, B), B)
        ref[k, rows, :] = ref[k, rows, :] * jnp.full((B, B), keep.astype(F32), F32).astype(BF)

    def mask_rows(srow, d):
        for i in range(4):
            for g in range(WIDTH):
                mask(d, g + i, i, xk[4 * srow + i, g])

    for copy in keeps + loads[:4]:
        copy.wait()
    mask_rows(l, dm)
    for copy in loads[4:]:
        copy.wait()
    mask_rows(1 - l, do)

    def cat(ref, base=0, count=4, rows=slice(None)):
        return jnp.concatenate([ref[base + j, rows, :] for j in range(count)], axis=1)

    def lhs(*pieces):
        return jnp.concatenate([cat(*p) for p in pieces], axis=1)

    def rhs(*pieces):
        return jnp.concatenate([cat(*p) for p in pieces], axis=0)

    def dot(a, b):
        return jnp.dot(a, b, preferred_element_type=F32)

    def put(ref, value):
        for j in range(value.shape[1] // B):
            ref[j] = value[:, j * B:(j + 1) * B]

    def store_y(dst, value, table, first, h, base=0, col=0, row=0):
        for i in range(row, row + value.shape[0] // B):
            for j in range(value.shape[1] // B):
                keep = table[first + i, jnp.clip(h + col + j - i, 0, 4 * W)].astype(F32) * scale
                block = value[(i - row) * B:(i - row + 1) * B, j * B:(j + 1) * B]
                dst[base + j, i * B:(i + 1) * B, :] = (block * keep).astype(BF)

    def to_sib(src, dst, index):
        return pltpu.make_async_remote_copy(src, dst, y_s.at[index], y_r.at[index], device_id=sib, device_id_type=MESH)

    send_ymo, send_ymp, send_ymm = to_sib(ymo, yom, 0), to_sib(ymp, yon, 1), to_sib(ymm, yoo, 2)
    mo, mm, mn = (dm, b_mo), (dm, 4), (dm, b_mn)
    theirs = 4 * (1 - l)
    z_out, c_out = NC * l, NZ * (1 - l)
    z_in, c_in = NC * (1 - l), NZ * l
    send_z = pltpu.make_async_remote_copy(zs, zr, z_s, z_r, device_id=facing, device_id_type=MESH)

    put(acc_mm, dot(lhs(mo, mm), rhs((do, b_om), mm)))
    zs[...] = acc_mm[z_out].astype(BF)
    store_y(ymo, dot(lhs(mo, mm), rhs((do, 4), mo)), yk, 4 * l, 12 - 8 * l)
    send_ymo.start()
    store_y(ymp, dot(cat(*mo), cat(do, b_op)), yk, 4 * l, 16 - 16 * l)
    send_ymp.start()

    put(acc_ymn, dot(cat(*mm), cat(*mn)))

    put(acc_mo, dot(cat(*mm), cat(ymo)))
    send_ymo.wait_recv()
    put(acc_o, dot(cat(*mo), cat(yom)))
    send_ymp.wait_recv()
    put(acc_mn, dot(cat(*mo), cat(yon)))

    @pl.when(has_n)
    def _():
        for copy in keys:
            copy.wait()

    to_smem = [pltpu.make_async_copy(xkv, xkn, k_sem.at[0]), pltpu.make_async_copy(ykv, ykn, k_sem.at[1])]
    for copy in to_smem:
        copy.start()
    for copy in to_smem:
        copy.wait()

    @pl.when(has_n)
    def _():
        send_z.start()

    def mask_tri(q):
        i, e = side(l == 0, q)
        for t in range(q + 1):
            mask(rnm, jnp.where(l == 0, 0, i) + t, i, xkn[theirs + i, e + t])

    @pl.when(has_n)
    def _():
        for copy in tri[1:]:
            copy.wait_recv()

    for q in range(1, 4):
        mask_tri(q)
    part = pl.ds(pl.multiple_of(c_out * B, B), NC * B)
    value = cat(acc_mm, c_out, NC) + dot(cat(dm, b_mn + c_out, NC), cat(rnm, c_out, NC, part))
    store_y(ymm, value, yk, 4 * l, 8, c_out, c_out)
    c = dot(cat(rnm, 0, 4, part), cat(ymm, c_out, NC))

    def pick(value, first, a, b):
        block = value[a * B:(a + 1) * B, b * B:(b + 1) * B]
        return block if a == b else jnp.where(first, block, value[b * B:(b + 1) * B, a * B:(a + 1) * B])

    for n, (a, b) in enumerate(PAIRS[:NP]):
        block = pick(c, l == 0, a, b).astype(BF)
        for h in range(2):
            cs[h, n] = block[h * HALF:(h + 1) * HALF]
    def send_c(src, dst, send, recv, there):
        return pltpu.make_async_remote_copy(src, dst, c_s.at[send], c_r.at[recv], device_id=there, device_id_type=MESH)

    c_facing = send_c(cs.at[1 - l], cm, 0, 0, facing)
    c_same = send_c(cs.at[l], co, 1, 1, same)
    c_late = send_c(cs.at[l], fw, 2, 2, facing)
    c_forward = send_c(fw, co, 3, 1, sib)

    @pl.when(jnp.logical_and(has_n, jnp.logical_not(early)))
    def _():
        c_same.start()

    @pl.when(early)
    def _():
        c_late.start()

    @pl.when(has_n)
    def _():
        c_facing.start()

    @pl.when(has_n)
    def _():
        tri[0].wait_recv()

    mask_tri(0)
    store_y(ymm, acc_mm[z_out] + dot(cat(*mn), rnm[z_out]), yk, 4 * l, 8, z_out, z_out)
    send_ymm.start()
    store_y(yno, dot(cat(rnm), cat(*mo)), ykn, theirs, 16 - 16 * l)
    put(acc_ynm, dot(cat(rnm), cat(*mm)))
    acc_z[...] = dot(cat(rnm), dm[b_mn + z_in])

    def finish(cube, base, i, j):
        keep = xk[4 * l + i, base + j - i].astype(F32)
        rows = pl.ds(i * B if isinstance(i, int) else pl.multiple_of(i * B, B), B)
        own = dm[base + j, rows, :].astype(F32)
        return ((1.5 * own - (0.5 * scale) * cube) * keep).astype(BF)

    def stage(cube, base, i, j):
        block = finish(cube, base, i, j)
        low, high = block[:HALF], block[HALF:]
        out_ref[4 * l + i, base + j - i] = jnp.where(l == 0, low, high)
        stg[i, base + j - i] = jnp.where(l == 0, high, low)

    def outs(n, i, e, count):
        return pltpu.make_async_remote_copy(
            stg.at[i, pl.ds(e, count)], out_ref.at[4 * l + i, pl.ds(e, count)], o_s.at[n], o_r.at[n],
            device_id=sib, device_id_type=MESH)

    put(acc_o, cat(acc_o) + dot(cat(*mm), cat(ymm)))
    send_ymm.wait_recv()
    value = cat(acc_mo) + dot(lhs(mo, mn), rhs((yoo,), (yno,)))
    for a, b in PAIRS:
        stage(pick(value, l == 0, a, b), b_mo, jnp.where(l == 0, a, b), jnp.where(l == 0, b, a))
    out_a = []
    for q in range(4):
        i, e = side(l == 0, q)
        out_a.append(outs(q, i, e, q + 1))
    for copy in out_a:
        copy.start()

    for first in (0, 2):
        rows = slice(first * B, (first + 2) * B)

        @pl.when(has_n)
        def _(first=first):
            for copy in mid[first:first + 2]:
                copy.wait_recv()

        for i in range(first, first + 2):
            for j in range(4):
                mask(rnn, j, i, xkn[theirs + i, 4 + j - i])
        part = cat(dm, b_mn + first, 2)
        value = cat(acc_ynm, 0, 4, rows) + dot(cat(rnn, 0, 4, rows), cat(rnm))
        store_y(ynm, value, ykn, theirs, 12 - 8 * l, row=first)
        value = cat(acc_o) + dot(part, cat(ynm, 0, 4, rows))
        if first == 0:
            put(acc_o, value)
            put(acc_ymn, cat(acc_ymn) + dot(part, cat(rnn, 0, 4, rows)))
    store_y(ymn, cat(acc_ymn) + dot(part, cat(rnn, 0, 4, rows)), yk, 4 * l, 4 + 8 * l)
    c_rows = pl.ds(pl.multiple_of(c_in * B, B), NC * B)
    part_c = cat(acc_mn, c_in, NC, c_rows) + dot(cat(dm, 4, 4, c_rows), cat(ymn, c_in, NC))
    for n, (a, b) in enumerate(PAIRS[:NP]):
        i, j = jnp.where(l == 1, NZ + a, b), jnp.where(l == 1, NZ + b, a)
        block = finish(pick(part_c, l == 1, a, b), b_mn, i, j)
        for h in range(2):
            pb[h, n] = block[h * HALF:(h + 1) * HALF]
    send_p = pltpu.make_async_remote_copy(pb.at[1 - l], po, p_s, p_r, device_id=sib, device_id_type=MESH)
    send_p.start()
    out_m = []
    for i in range(4):
        for j in range(4):
            stage(value[i * B:(i + 1) * B, j * B:(j + 1) * B], 4, i, j)
        out_m.append(outs(4 + i, i, 4 - i, 4))
        out_m[i].start()
    value = acc_mn[z_in] + dot(cat(*mm), ymn[z_in])

    @pl.when(has_n)
    def _():
        send_z.wait_recv()

    store_y(yz, zr[...].astype(F32) + acc_z[...], ykn, theirs, 8, 0, z_in)
    value = value + dot(cat(*mn), yz[0])
    out_z = []
    for i in range(4):
        stage(value[i * B:(i + 1) * B], b_mn, i, z_in)
        out_z.append(outs(8 + i, i, b_mn + z_in - i, 1))
        out_z[i].start()

    send_p.wait_recv()

    def add(srow, part, term):
        for n, (a, b) in enumerate(PAIRS[:NP]):
            i = jnp.where(srow == 1, NZ + a, b)
            e = jnp.where(srow == 1, 2 * W + b - a, a - b)
            keep = xk[4 * srow + i, e].astype(F32) * (0.5 * scale)
            out_ref[4 * srow + i, e] = (part[n].astype(F32) - keep * term[n].astype(F32)).astype(BF)

    @pl.when(late)
    def _():
        c_late.wait_recv()
        c_forward.start()

    @pl.when(has_n)
    def _():
        c_facing.wait_recv()

    add(l, pb.at[l], cm)

    @pl.when(has_other)
    def _():
        c_same.wait_recv()

    add(1 - l, po, co)

    for copy in out_a + out_m + out_z:
        copy.wait()
    for copy in (send_ymo, send_ymp, send_ymm, send_p):
        copy.wait_send()

    @pl.when(has_n)
    def _():
        for copy in tri + [send_z, c_facing]:
            copy.wait_send()

    @pl.when(early)
    def _():
        c_late.wait_send()

    @pl.when(jnp.logical_and(has_n, jnp.logical_not(early)))
    def _():
        c_same.wait_send()

    @pl.when(late)
    def _():
        c_forward.wait_send()

    @pl.when(has_n)
    def _():
        for copy in mid:
            copy.wait_send()


def solution(mesh):
    cols = mesh.shape["col"]
    groups = mesh.shape["row"] * cols

    def step(xband, xkeep, ykeep):
        scale = (2.0 * WIDTH * B) ** -0.5
        rows = xband.shape[0]
        dense = lambda n, dtype=BF: pltpu.VMEM((n, SUPER, B), dtype)
        sems = lambda *n: pltpu.SemaphoreType.DMA(n)
        halves = lambda *n: pltpu.VMEM((*n, HALF, B), BF)
        scratch = (
            [dense(12), dense(12)] + [dense(4)] * 11 + [dense(4, F32)] * 6
            + [pltpu.VMEM((SUPER, B), F32), pltpu.VMEM((SUPER, B), BF), pltpu.VMEM((SUPER, B), BF), dense(1)]
            + [halves(2, NP), halves(NP), halves(NP), halves(NP), halves(4, WIDTH), halves(2, NP), halves(NP)]
            + [pltpu.SMEM(a.shape, jnp.int32) for a in (xkeep, ykeep, xkeep, ykeep)]
            + [pltpu.VMEM(a.shape, jnp.int32) for a in (xkeep, ykeep)]
            + [sems(2, 4), sems(2), sems(4), sems(4), sems(4), sems(4), sems(2), sems(2), sems(3), sems(3)]
            + [sems(), sems(), sems(4), sems(3), sems(12), sems(12), sems(), sems()]
        )
        args = [pltpu.with_memory_space_constraint(a, pltpu.HBM) for a in (xband, xkeep, ykeep)]
        return pl.pallas_call(
            functools.partial(kernel, groups, cols, scale),
            out_shape=jax.ShapeDtypeStruct((rows, WIDTH, HALF, B), BF),
            in_specs=[pl.BlockSpec(memory_space=pl.ANY)] * 3,
            out_specs=pl.BlockSpec(memory_space=pltpu.VMEM),
            scratch_shapes=scratch,
            compiler_params=pltpu.CompilerParams(
                collective_id=0, has_side_effects=True, vmem_limit_bytes=40 * 2**20),
        )(*args)

    in_specs = (P(("row", "col"), None, None, None), P(("row", "col"), None), P(("row", "col"), None))
    return jax.shard_map(step, mesh=mesh, in_specs=in_specs, out_specs=P(("row", "col"), None, "layer", None), check_vma=False)
```

```python
import functools

import jax
import jax.numpy as jnp
from jax import lax
from jax.experimental import pallas as pl
from jax.experimental.pallas import tpu as pltpu
from jax.sharding import PartitionSpec as P

B = 128
W = 4
LAST = 7
NC = 3
NZ = W - NC
PAIRS = [(a, b) for a in range(W) for b in range(a + 1)]
NP = NC * (NC + 1) // 2
WIDTH = 2 * W + 1
SUPER = W * B
HALF = B // 2
MESH = pl.DeviceIdType.MESH
BF = jnp.bfloat16
F32 = jnp.float32


def kernel(
    groups, cols, scale,
    x_hbm, xk_hbm, yk_hbm, out_ref,
    dm, do, rnm, rnn, ymo, ymm, ymp, yom, yoo, yon, ynm, yno, ymn,
    acc_mm, acc_mn, acc_o, acc_mo, acc_ynm, acc_ymn, acc_z, zs, zr, yz, cs, cm, co, fw, stg, pb, po, xk, yk, xkn, ykn, xkv, ykv,
    in_sem, k_sem, tri_s, tri_r, mid_s, mid_r, key_s, key_r, y_s, y_r, z_s, z_r, c_s, c_r,
    o_s, o_r, p_s, p_r,
):
    row, col, l = lax.axis_index("row"), lax.axis_index("col"), lax.axis_index("layer")
    group = row * cols + col
    step = 2 * l - 1

    def device(g, layer):
        g = lax.rem(g + groups, groups)
        return (g // cols, lax.rem(g, cols), layer)

    sib = (row, col, 1 - l)
    facing = device(group + step, 1 - l)
    same = device(group + step, l)
    other = device(group - step, l)
    has_n = jnp.logical_and(group + step >= 0, group + step < groups)
    has_other = jnp.logical_and(group - step >= 0, group - step < groups)

    early = jnp.logical_and(has_n, jnp.logical_and(l == 0, lax.rem(col, LAST + 1) == 0))
    beside_late = jnp.logical_and(l == 0, lax.rem(col, LAST + 1) == LAST)
    late = jnp.logical_and(has_n, jnp.logical_and(l == 1, lax.rem(col, LAST + 1) == LAST))

    barrier = pltpu.get_barrier_semaphore()
    pl.semaphore_signal(barrier, inc=1, device_id=sib, device_id_type=MESH)

    @pl.when(has_n)
    def _():
        pl.semaphore_signal(barrier, inc=1, device_id=facing, device_id_type=MESH)

    @pl.when(jnp.logical_and(has_other, jnp.logical_not(beside_late)))
    def _():
        pl.semaphore_signal(barrier, inc=1, device_id=other, device_id_type=MESH)

    b_mo, b_mn, b_om, b_op = 8 * (1 - l), 8 * l, 8 * l, 8 * (1 - l)

    def side(right, q):
        return jnp.where(right, q, 3 - q), jnp.where(right, 8 - q, 0)

    keeps = [pltpu.make_async_copy(xk_hbm, xk, k_sem.at[0]), pltpu.make_async_copy(yk_hbm, yk, k_sem.at[1])]
    loads = [
        pltpu.make_async_copy(x_hbm.at[4 * s + i], d.at[pl.ds(i, WIDTH), pl.ds(i * B, B)], in_sem.at[n, i])
        for n, (s, d) in enumerate(((l, dm), (1 - l, do)))
        for i in range(4)
    ]
    @pl.when(jnp.logical_not(late))
    def _():
        for copy in keeps + loads:
            copy.start()

    keys = [
        pltpu.make_async_remote_copy(src, dst, key_s.at[n], key_r.at[n], device_id=facing, device_id_type=MESH)
        for n, (src, dst) in enumerate(((xk_hbm, xkv), (yk_hbm, ykv)))
    ]
    tri, mid = [], []
    for q in range(4):
        i, e = side(l == 1, q)
        rows = pl.ds(pl.multiple_of(i * B, B), B)
        tri.append(pltpu.make_async_remote_copy(
            x_hbm.at[4 * l + i, pl.ds(e, q + 1)], rnm.at[pl.ds(jnp.where(l == 1, 0, i), q + 1), rows],
            tri_s.at[q], tri_r.at[q], device_id=facing, device_id_type=MESH))
    for i in range(4):
        mid.append(pltpu.make_async_remote_copy(
            x_hbm.at[4 * l + i, pl.ds(4 - i, 4)], rnn.at[:, pl.ds(i * B, B)],
            mid_s.at[i], mid_r.at[i], device_id=facing, device_id_type=MESH))

    @pl.when(jnp.logical_not(has_n))
    def _():
        rnm[...] = jnp.zeros_like(rnm)
        rnn[...] = jnp.zeros_like(rnn)
        zr[...] = jnp.zeros_like(zr)
        cm[...] = jnp.zeros_like(cm)
        xkv[...] = jnp.zeros_like(xkv)
        ykv[...] = jnp.zeros_like(ykv)

    @pl.when(jnp.logical_not(has_other))
    def _():
        co[...] = jnp.zeros_like(co)

    pl.semaphore_wait(barrier, jnp.where(has_n, jnp.where(early, 2, 3), 1))

    @pl.when(has_n)
    def _():
        for copy in tri[3:] + keys + tri[2::-1] + mid:
            copy.start()

    @pl.when(late)
    def _():
        for copy in keeps + loads:
            copy.start()

    for d in (dm, do):
        for k in range(3):
            d[k, (k + 1) * B:, :] = jnp.zeros((SUPER - (k + 1) * B, B), BF)
            d[9 + k, : (k + 1) * B, :] = jnp.zeros(((k + 1) * B, B), BF)
    for s in range(1, 4):
        k = jnp.where(l == 1, s - 1, 4 - s)
        start = pl.multiple_of(jnp.where(l == 1, s * B, 0), B)
        rnm[k, pl.ds(start, (4 - s) * B), :] = jnp.zeros(((4 - s) * B, B), BF)

    def mask(ref, k, i, keep):
        rows = pl.ds(i * B if isinstance(i, int) else pl.multiple_of(i * B, B), B)
        ref[k, rows, :] = ref[k, rows, :] * jnp.full((B, B), keep.astype(F32), F32).astype(BF)

    def mask_rows(srow, d):
        for i in range(4):
            for g in range(WIDTH):
                mask(d, g + i, i, xk[4 * srow + i, g])

    for copy in keeps + loads[:4]:
        copy.wait()
    mask_rows(l, dm)
    for copy in loads[4:]:
        copy.wait()
    mask_rows(1 - l, do)

    def cat(ref, base=0, count=4, rows=slice(None)):
        return jnp.concatenate([ref[base + j, rows, :] for j in range(count)], axis=1)

    def lhs(*pieces):
        return jnp.concatenate([cat(*p) for p in pieces], axis=1)

    def rhs(*pieces):
        return jnp.concatenate([cat(*p) for p in pieces], axis=0)

    def dot(a, b):
        return jnp.dot(a, b, preferred_element_type=F32)

    def put(ref, value):
        for j in range(value.shape[1] // B):
            ref[j] = value[:, j * B:(j + 1) * B]

    def store_y(dst, value, table, first, h, base=0, col=0, row=0):
        for i in range(row, row + value.shape[0] // B):
            for j in range(value.shape[1] // B):
                keep = table[first + i, jnp.clip(h + col + j - i, 0, 4 * W)].astype(F32) * scale
                block = value[(i - row) * B:(i - row + 1) * B, j * B:(j + 1) * B]
                dst[base + j, i * B:(i + 1) * B, :] = (block * keep).astype(BF)

    def to_sib(src, dst, index):
        return pltpu.make_async_remote_copy(src, dst, y_s.at[index], y_r.at[index], device_id=sib, device_id_type=MESH)

    send_ymo, send_ymp, send_ymm = to_sib(ymo, yom, 0), to_sib(ymp, yon, 1), to_sib(ymm, yoo, 2)
    mo, mm, mn = (dm, b_mo), (dm, 4), (dm, b_mn)
    theirs = 4 * (1 - l)
    z_out, c_out = NC * l, NZ * (1 - l)
    z_in, c_in = NC * (1 - l), NZ * l
    send_z = pltpu.make_async_remote_copy(zs, zr, z_s, z_r, device_id=facing, device_id_type=MESH)

    put(acc_mm, dot(lhs(mo, mm), rhs((do, b_om), mm)))
    zs[...] = acc_mm[z_out].astype(BF)
    store_y(ymo, dot(lhs(mo, mm), rhs((do, 4), mo)), yk, 4 * l, 12 - 8 * l)
    send_ymo.start()
    store_y(ymp, dot(cat(*mo), cat(do, b_op)), yk, 4 * l, 16 - 16 * l)
    send_ymp.start()

    put(acc_ymn, dot(cat(*mm), cat(*mn)))

    put(acc_mo, dot(cat(*mm), cat(ymo)))
    send_ymo.wait_recv()
    put(acc_o, dot(cat(*mo), cat(yom)))
    send_ymp.wait_recv()
    put(acc_mn, dot(cat(*mo), cat(yon)))

    @pl.when(has_n)
    def _():
        for copy in keys:
            copy.wait()

    to_smem = [pltpu.make_async_copy(xkv, xkn, k_sem.at[0]), pltpu.make_async_copy(ykv, ykn, k_sem.at[1])]
    for copy in to_smem:
        copy.start()
    for copy in to_smem:
        copy.wait()

    @pl.when(has_n)
    def _():
        send_z.start()

    def mask_tri(q):
        i, e = side(l == 0, q)
        for t in range(q + 1):
            mask(rnm, jnp.where(l == 0, 0, i) + t, i, xkn[theirs + i, e + t])

    @pl.when(has_n)
    def _():
        for copy in tri[1:]:
            copy.wait_recv()

    for q in range(1, 4):
        mask_tri(q)
    part = pl.ds(pl.multiple_of(c_out * B, B), NC * B)
    value = cat(acc_mm, c_out, NC) + dot(cat(dm, b_mn + c_out, NC), cat(rnm, c_out, NC, part))
    store_y(ymm, value, yk, 4 * l, 8, c_out, c_out)
    c = dot(cat(rnm, 0, 4, part), cat(ymm, c_out, NC))

    def pick(value, first, a, b):
        block = value[a * B:(a + 1) * B, b * B:(b + 1) * B]
        return block if a == b else jnp.where(first, block, value[b * B:(b + 1) * B, a * B:(a + 1) * B])

    for n, (a, b) in enumerate(PAIRS[:NP]):
        block = pick(c, l == 0, a, b).astype(BF)
        for h in range(2):
            cs[h, n] = block[h * HALF:(h + 1) * HALF]
    def send_c(src, dst, send, recv, there):
        return pltpu.make_async_remote_copy(src, dst, c_s.at[send], c_r.at[recv], device_id=there, device_id_type=MESH)

    c_facing = send_c(cs.at[1 - l], cm, 0, 0, facing)
    c_same = send_c(cs.at[l], co, 1, 1, same)
    c_late = send_c(cs.at[l], fw, 2, 2, facing)
    c_forward = send_c(fw, co, 3, 1, sib)

    @pl.when(jnp.logical_and(has_n, jnp.logical_not(early)))
    def _():
        c_same.start()

    @pl.when(early)
    def _():
        c_late.start()

    @pl.when(has_n)
    def _():
        c_facing.start()

    @pl.when(has_n)
    def _():
        tri[0].wait_recv()

    mask_tri(0)
    store_y(ymm, acc_mm[z_out] + dot(cat(*mn), rnm[z_out]), yk, 4 * l, 8, z_out, z_out)
    send_ymm.start()
    store_y(yno, dot(cat(rnm), cat(*mo)), ykn, theirs, 16 - 16 * l)
    put(acc_ynm, dot(cat(rnm), cat(*mm)))
    acc_z[...] = dot(cat(rnm), dm[b_mn + z_in])

    def finish(cube, base, i, j):
        keep = xk[4 * l + i, base + j - i].astype(F32)
        rows = pl.ds(i * B if isinstance(i, int) else pl.multiple_of(i * B, B), B)
        own = dm[base + j, rows, :].astype(F32)
        return ((1.5 * own - (0.5 * scale) * cube) * keep).astype(BF)

    def stage(cube, base, i, j):
        block = finish(cube, base, i, j)
        low, high = block[:HALF], block[HALF:]
        out_ref[4 * l + i, base + j - i] = jnp.where(l == 0, low, high)
        stg[i, base + j - i] = jnp.where(l == 0, high, low)

    def outs(n, i, e, count):
        return pltpu.make_async_remote_copy(
            stg.at[i, pl.ds(e, count)], out_ref.at[4 * l + i, pl.ds(e, count)], o_s.at[n], o_r.at[n],
            device_id=sib, device_id_type=MESH)

    put(acc_o, cat(acc_o) + dot(cat(*mm), cat(ymm)))
    send_ymm.wait_recv()
    value = cat(acc_mo) + dot(lhs(mo, mn), rhs((yoo,), (yno,)))
    for a, b in PAIRS:
        stage(pick(value, l == 0, a, b), b_mo, jnp.where(l == 0, a, b), jnp.where(l == 0, b, a))
    out_a = []
    for q in range(4):
        i, e = side(l == 0, q)
        out_a.append(outs(q, i, e, q + 1))
    for copy in out_a:
        copy.start()

    for first in (0, 2):
        rows = slice(first * B, (first + 2) * B)

        @pl.when(has_n)
        def _(first=first):
            for copy in mid[first:first + 2]:
                copy.wait_recv()

        for i in range(first, first + 2):
            for j in range(4):
                mask(rnn, j, i, xkn[theirs + i, 4 + j - i])
        part = cat(dm, b_mn + first, 2)
        value = cat(acc_ynm, 0, 4, rows) + dot(cat(rnn, 0, 4, rows), cat(rnm))
        store_y(ynm, value, ykn, theirs, 12 - 8 * l, row=first)
        value = cat(acc_o) + dot(part, cat(ynm, 0, 4, rows))
        if first == 0:
            put(acc_o, value)
            put(acc_ymn, cat(acc_ymn) + dot(part, cat(rnn, 0, 4, rows)))
    store_y(ymn, cat(acc_ymn) + dot(part, cat(rnn, 0, 4, rows)), yk, 4 * l, 4 + 8 * l)
    c_rows = pl.ds(pl.multiple_of(c_in * B, B), NC * B)
    part_c = cat(acc_mn, c_in, NC, c_rows) + dot(cat(dm, 4, 4, c_rows), cat(ymn, c_in, NC))
    for n, (a, b) in enumerate(PAIRS[:NP]):
        i, j = jnp.where(l == 1, NZ + a, b), jnp.where(l == 1, NZ + b, a)
        block = finish(pick(part_c, l == 1, a, b), b_mn, i, j)
        for h in range(2):
            pb[h, n] = block[h * HALF:(h + 1) * HALF]
    send_p = pltpu.make_async_remote_copy(pb.at[1 - l], po, p_s, p_r, device_id=sib, device_id_type=MESH)
    send_p.start()
    out_m = []
    for i in range(4):
        for j in range(4):
            stage(value[i * B:(i + 1) * B, j * B:(j + 1) * B], 4, i, j)
        out_m.append(outs(4 + i, i, 4 - i, 4))
        out_m[i].start()
    value = acc_mn[z_in] + dot(cat(*mm), ymn[z_in])

    @pl.when(has_n)
    def _():
        send_z.wait_recv()

    store_y(yz, zr[...].astype(F32) + acc_z[...], ykn, theirs, 8, 0, z_in)
    value = value + dot(cat(*mn), yz[0])
    out_z = []
    for i in range(4):
        stage(value[i * B:(i + 1) * B], b_mn, i, z_in)
        out_z.append(outs(8 + i, i, b_mn + z_in - i, 1))
        out_z[i].start()

    send_p.wait_recv()

    def add(srow, part, term):
        for n, (a, b) in enumerate(PAIRS[:NP]):
            i = jnp.where(srow == 1, NZ + a, b)
            e = jnp.where(srow == 1, 2 * W + b - a, a - b)
            keep = xk[4 * srow + i, e].astype(F32) * (0.5 * scale)
            out_ref[4 * srow + i, e] = (part[n].astype(F32) - keep * term[n].astype(F32)).astype(BF)

    @pl.when(late)
    def _():
        c_late.wait_recv()
        c_forward.start()

    @pl.when(has_n)
    def _():
        c_facing.wait_recv()

    add(l, pb.at[l], cm)

    @pl.when(has_other)
    def _():
        c_same.wait_recv()

    add(1 - l, po, co)

    for copy in out_a + out_m + out_z:
        copy.wait()
    for copy in (send_ymo, send_ymp, send_ymm, send_p):
        copy.wait_send()

    @pl.when(has_n)
    def _():
        for copy in tri + [send_z, c_facing]:
            copy.wait_send()

    @pl.when(early)
    def _():
        c_late.wait_send()

    @pl.when(jnp.logical_and(has_n, jnp.logical_not(early)))
    def _():
        c_same.wait_send()

    @pl.when(late)
    def _():
        c_forward.wait_send()

    @pl.when(has_n)
    def _():
        for copy in mid:
            copy.wait_send()


def solution(mesh):
    cols = mesh.shape["col"]
    groups = mesh.shape["row"] * cols

    def step(xband, xkeep, ykeep):
        scale = (2.0 * WIDTH * B) ** -0.5
        rows = xband.shape[0]
        dense = lambda n, dtype=BF: pltpu.VMEM((n, SUPER, B), dtype)
        sems = lambda *n: pltpu.SemaphoreType.DMA(n)
        halves = lambda *n: pltpu.VMEM((*n, HALF, B), BF)
        scratch = (
            [dense(12), dense(12)] + [dense(4)] * 11 + [dense(4, F32)] * 6
            + [pltpu.VMEM((SUPER, B), F32), pltpu.VMEM((SUPER, B), BF), pltpu.VMEM((SUPER, B), BF), dense(1)]
            + [halves(2, NP), halves(NP), halves(NP), halves(NP), halves(4, WIDTH), halves(2, NP), halves(NP)]
            + [pltpu.SMEM(a.shape, jnp.int32) for a in (xkeep, ykeep, xkeep, ykeep)]
            + [pltpu.VMEM(a.shape, jnp.int32) for a in (xkeep, ykeep)]
            + [sems(2, 4), sems(2), sems(4), sems(4), sems(4), sems(4), sems(2), sems(2), sems(3), sems(3)]
            + [sems(), sems(), sems(4), sems(3), sems(12), sems(12), sems(), sems()]
        )
        args = [pltpu.with_memory_space_constraint(a, pltpu.HBM) for a in (xband, xkeep, ykeep)]
        return pl.pallas_call(
            functools.partial(kernel, groups, cols, scale),
            out_shape=jax.ShapeDtypeStruct((rows, WIDTH, HALF, B), BF),
            in_specs=[pl.BlockSpec(memory_space=pl.ANY)] * 3,
            out_specs=pl.BlockSpec(memory_space=pltpu.VMEM),
            scratch_shapes=scratch,
            compiler_params=pltpu.CompilerParams(
                collective_id=0, has_side_effects=True, vmem_limit_bytes=40 * 2**20),
        )(*args)

    in_specs = (P(("row", "col"), None, None, None), P(("row", "col"), None), P(("row", "col"), None))
    return jax.shard_map(step, mesh=mesh, in_specs=in_specs, out_specs=P(("row", "col"), None, "layer", None), check_vma=False)
```
